32 devices in a mesh: fsdp: 4 (over z), ep: 8 (over y, x, core).
Axes of the slice: x: 2, y: 2, z: 4, core: 2. Of those that a mesh axis runs over, the one named last changes fastest.
Arguments:
- deltas: bfloat16 [8, 7168, 2048], P('ep', 'fsdp')
- sketch_matrix: bfloat16 [2048, 256], replicated, may hold values from -0.125 to 0.125
- owner_of: int32 [8], replicated, may hold values from 0 to 7, as said below
- serving: bfloat16 [16, 7168, 2048], P('ep', 'fsdp'), may hold values from -4 to 4
Outputs:
- updated: bfloat16 [16, 7168, 2048], P('ep', 'fsdp')
The draws below stay inside these ranges and needn't reach their ends.
Inputs may be any that keep to these rules, and one draw needn't show every extreme that they name: `owner_of`: each of the 8 owners owns at most 2 experts; in every draw some owner owns exactly 2 and some own none.
All inputs are finite; a program needn't handle non-finite values.
Results may differ from the reference program's by a relative error of at most 0.007.
Values may be sent and summed in bfloat16 or wider, within the bound.
A program may use at most 128 MiB of HBM per device.

```python
import jax
import jax.numpy as jnp
from jax import lax

D = 7168
FF = 2048
RANK = 256
POWER = 2
SLOTS = 2
EXPERTS = 8
N_EP = 8


def draw_deltas(key, part):
    base = jax.random.fold_in(key, 23)
    values = jnp.clip(jax.random.normal(base, (EXPERTS, D, FF), jnp.float32), -6.0, 6.0)
    return values.astype(jnp.bfloat16)


def draw_owner_of(key, part):
    base = jax.random.fold_in(key, 11)
    key_pairs, key_owners, key_order, key_experts = jax.random.split(base, 4)
    total = EXPERTS
    paired = jax.random.randint(key_pairs, (), 1, total // 2 + 1)
    position = jnp.arange(total, dtype=jnp.int32)
    middle = (1 + jax.random.permutation(key_owners, total - 2)).astype(jnp.int32)
    candidates = jnp.concatenate([jnp.array([0, total - 1], jnp.int32), middle])
    scores = jax.random.permutation(key_order, total).astype(jnp.int32)
    scores = scores + jnp.where(position < total - paired, 0, total).astype(jnp.int32)
    order = jnp.argsort(scores, stable=True)
    owner_perm = candidates[order]
    source = jnp.where(position < 2 * paired, position // 2, position - paired)
    assigned = owner_perm[source].astype(jnp.int32)
    expert_perm = jax.random.permutation(key_experts, total)
    return jnp.zeros((total,), jnp.int32).at[expert_perm].set(assigned)


def block_levels(own_key, extent, pieces, least, top_value):
    loudness, own = 1.0, jax.random.fold_in(own_key, 6)
    for dim, shards_of in pieces:
        steps = jnp.exp(jax.random.uniform(jax.random.fold_in(own, dim), (shards_of,), jnp.float32, least / len(pieces), top_value / len(pieces)))
        loudness = loudness * jnp.repeat(steps, extent[dim] // shards_of).reshape([-1 if axis == dim else 1 for axis in range(len(extent))])
    return loudness


def scatter_about(rng, shape, width, reach, cuts=(), kind=jnp.bfloat16):
    drawn = jax.random.normal(rng, shape, jnp.float32) * width
    if len(cuts) > 0:
        drawn = block_levels(rng, shape, cuts, -0.22, 0.18) * drawn
    return jnp.clip(drawn, min=-reach, max=reach).astype(kind)


def setup_inputs(seed: int = 0) -> dict:
    keys = jax.random.split(jax.random.key(seed), 5)
    return {
        "deltas": draw_deltas(jax.random.fold_in(keys[4], 71), 0),
        "sketch_matrix": scatter_about(keys[1], (FF, RANK), FF ** -0.5, 0.125),
        "owner_of": draw_owner_of(jax.random.fold_in(keys[4], 71), 0),
        "serving": scatter_about(keys[3], (N_EP * SLOTS, D, FF), 0.5, 4.0, ((0, 8), (1, 4))),
    }


def sketch_one(delta_one, sketch_matrix):
    contract = (((0,), (0,)), ((), ()))
    current = jnp.dot(delta_one.astype(jnp.float32), sketch_matrix.astype(jnp.float32), preferred_element_type=jnp.float32).astype(jnp.bfloat16)
    for iteration in range(POWER):
        power_step = lax.dot_general(delta_one.astype(jnp.float32), current.astype(jnp.float32), contract, preferred_element_type=jnp.float32)
        power_step = (power_step / D).astype(jnp.bfloat16)
        current = jnp.dot(delta_one.astype(jnp.float32), power_step.astype(jnp.float32), preferred_element_type=jnp.float32).astype(jnp.bfloat16)
    gram_total = lax.dot_general(current.astype(jnp.float32), current.astype(jnp.float32), contract, preferred_element_type=jnp.float32)
    cross_total = lax.dot_general(current.astype(jnp.float32), delta_one.astype(jnp.float32), contract, preferred_element_type=jnp.float32)
    factor_low = jnp.linalg.cholesky(gram_total)
    basis_rows = lax.linalg.triangular_solve(factor_low, current.astype(jnp.float32).T, left_side=True, lower=True)
    coeffs = lax.linalg.triangular_solve(factor_low, cross_total, left_side=True, lower=True)
    return (basis_rows.astype(jnp.bfloat16), coeffs.astype(jnp.bfloat16))

def reference(deltas, sketch_matrix, owner_of, serving):
    basis_all, coeff_all = lax.map(lambda delta_one: sketch_one(delta_one, sketch_matrix), deltas)
    expert_ids = jnp.arange(EXPERTS, dtype=jnp.int32)

    def rebuild(slot_index):
        owner_now = slot_index // SLOTS
        place_now = slot_index % SLOTS
        is_owned = (owner_of == owner_now).astype(jnp.int32)
        owned_rank = jnp.cumsum(is_owned, dtype=jnp.int32) - 1
        slot_hits = (is_owned == 1) & (owned_rank == place_now)
        present = jnp.any(slot_hits)
        chosen = jnp.sum(jnp.where(slot_hits, expert_ids, 0)).astype(jnp.int32)
        update = lax.dot_general(basis_all[chosen].astype(jnp.float32), coeff_all[chosen].astype(jnp.float32), (((0,), (0,)), ((), ())), preferred_element_type=jnp.float32)
        summed = serving[slot_index].astype(jnp.float32) + jnp.where(present, update, jnp.float32(0.0))
        return summed.astype(jnp.bfloat16)
    return lax.map(rebuild, jnp.arange(N_EP * SLOTS, dtype=jnp.int32))
```

```python
import functools

import jax
import jax.numpy as jnp
from jax import lax
from jax.experimental import pallas as pl
from jax.experimental.pallas import tpu as pltpu
from jax.sharding import PartitionSpec as P

D = 7168
POWER = 2
MESH = pl.DeviceIdType.MESH
CHUNK = 256
SKEW = 2
VMEM_LIMIT = 56 * 1024 * 1024
F32 = jnp.float32
BF16 = jnp.bfloat16


def greet(me, n):
    barrier = pltpu.get_barrier_semaphore()

    @pl.when(me > 0)
    def _():
        pl.semaphore_signal(barrier, inc=1, device_id={"fsdp": me - 1}, device_id_type=MESH)

    @pl.when(me < n - 1)
    def _():
        pl.semaphore_signal(barrier, inc=1, device_id={"fsdp": me + 1}, device_id_type=MESH)

    peers = (me > 0).astype(jnp.int32) + (me < n - 1).astype(jnp.int32)
    pl.semaphore_wait(barrier, peers)


def chain_sum(me, n, chunks, part, compute, emit, bufs, ssem, rsem):
    send_r, send_l, recv_l, recv_r = bufs
    lower = me < n // 2

    def to_right(j):
        return pltpu.make_async_remote_copy(
            src_ref=send_r.at[j], dst_ref=recv_l.at[j], send_sem=ssem.at[0, j],
            recv_sem=rsem.at[0, j], device_id={"fsdp": jnp.minimum(me + 1, n - 1)}, device_id_type=MESH)

    def to_left(j):
        return pltpu.make_async_remote_copy(
            src_ref=send_l.at[j], dst_ref=recv_r.at[j], send_sem=ssem.at[1, j],
            recv_sem=rsem.at[1, j], device_id={"fsdp": jnp.maximum(me - 1, 0)}, device_id_type=MESH)

    @pl.when(me == 0)
    def _():
        recv_l[...] = jnp.zeros_like(recv_l)

    @pl.when(me == n - 1)
    def _():
        recv_r[...] = jnp.zeros_like(recv_r)

    def rightward(j):
        @pl.when(me > 0)
        def _():
            to_right(j).wait_recv()

        @pl.when(me < n - 1)
        def _():
            send_r[j] = (part[j] + recv_l[j].astype(F32)).astype(send_r.dtype)
            to_right(j).start()

    def leftward(j):
        @pl.when(me < n - 1)
        def _():
            to_left(j).wait_recv()

        @pl.when(me > 0)
        def _():
            send_l[j] = (part[j] + recv_r[j].astype(F32)).astype(send_l.dtype)
            to_left(j).start()

    def step(t, carry):
        @pl.when(t < chunks)
        def _():
            part[t] = compute(t)

            @pl.when(lower)
            def _():
                rightward(t)

            @pl.when(jnp.logical_not(lower))
            def _():
                leftward(t)

        @pl.when(t >= SKEW)
        def _():
            j = t - SKEW

            @pl.when(lower)
            def _():
                leftward(j)

            @pl.when(jnp.logical_not(lower))
            def _():
                rightward(j)

            emit(j, part[j] + recv_l[j].astype(F32) + recv_r[j].astype(F32))

        return carry

    lax.fori_loop(0, chunks + SKEW, step, 0)

    def drain(j, carry):
        @pl.when(me < n - 1)
        def _():
            to_right(j).wait_send()

        @pl.when(me > 0)
        def _():
            to_left(j).wait_send()

        return carry

    lax.fori_loop(0, chunks, drain, 0)


def power_kernel(n, tile, chunks, a_ref, w_ref, y_ref, yt, p, part, send_r, send_l, recv_l, recv_r, ssem, rsem):
    me = lax.axis_index("fsdp")
    rows = a_ref.shape[0]
    greet(me, n)

    def sketch(weights):
        def body(i, carry):
            at = pl.ds(pl.multiple_of(i * tile, tile), tile)
            block = jnp.dot(a_ref[at, :], weights[...], preferred_element_type=F32)
            y_ref[at, :] = block.astype(BF16)
            yt[:, at] = block.T.astype(BF16)
            return carry

        lax.fori_loop(0, rows // tile, body, 0)

    def compute(j):
        at = pl.ds(pl.multiple_of(j * CHUNK, CHUNK), CHUNK)
        return jnp.dot(yt[...], a_ref[:, at], preferred_element_type=F32)

    def emit(j, total):
        at = pl.ds(pl.multiple_of(j * CHUNK, CHUNK), CHUNK)
        p[at, :] = (total / D).T.astype(BF16)

    sketch(w_ref)
    for i in range(POWER):
        bufs = [b.at[i] for b in (send_r, send_l, recv_l, recv_r)]
        chain_sum(me, n, chunks, part, compute, emit, bufs, ssem.at[i], rsem.at[i])
        sketch(p)


def power_call(n, deltas, weights):
    rows, ff = deltas.shape
    rank = weights.shape[1]
    tile = 256 if rows % 256 == 0 else 128
    chunks = ff // CHUNK
    comm = pltpu.VMEM((POWER, chunks, rank, CHUNK), BF16)
    vmem = pl.BlockSpec(memory_space=pltpu.VMEM)
    return pl.pallas_call(
        functools.partial(power_kernel, n, tile, chunks),
        out_shape=jax.ShapeDtypeStruct((rows, rank), BF16),
        in_specs=[vmem, vmem],
        out_specs=vmem,
        scratch_shapes=[
            pltpu.VMEM((rank, rows), BF16),
            pltpu.VMEM((ff, rank), BF16),
            pltpu.VMEM((chunks, rank, CHUNK), F32),
            comm, comm, comm, comm,
            pltpu.SemaphoreType.DMA((POWER, 2, chunks)),
            pltpu.SemaphoreType.DMA((POWER, 2, chunks)),
        ],
        compiler_params=pltpu.CompilerParams(
            collective_id=0, has_side_effects=True, vmem_limit_bytes=VMEM_LIMIT),
        cost_estimate=pl.CostEstimate(
            flops=2 * rows * ff * rank * 5, bytes_accessed=rows * ff * 2, transcendentals=0),
        name="power_steps",
    )(deltas, weights)


def cross_kernel(n, tile, chunks, a_ref, y_ref, gram_ref, cross_ref, yt, part, gpart,
                 gsend_r, gsend_l, grecv_l, grecv_r, send_r, send_l, recv_l, recv_r,
                 gssem, grsem, ssem, rsem):
    me = lax.axis_index("fsdp")
    rows = a_ref.shape[0]
    share = chunks // n
    greet(me, n)

    def turn(i, carry):
        at = pl.ds(pl.multiple_of(i * tile, tile), tile)
        yt[:, at] = y_ref[at, :].astype(F32).T.astype(BF16)
        return carry

    lax.fori_loop(0, rows // tile, turn, 0)

    def compute(j):
        at = pl.ds(pl.multiple_of(j * CHUNK, CHUNK), CHUNK)
        return jnp.dot(yt[...], a_ref[:, at], preferred_element_type=F32)

    def emit(j, total):
        @pl.when((j >= me * share) & (j < (me + 1) * share))
        def _():
            at = pl.ds(pl.multiple_of((j - me * share) * CHUNK, CHUNK), CHUNK)
            cross_ref[:, at] = total

    def gcompute(j):
        return jnp.dot(yt[...], y_ref[...], preferred_element_type=F32)

    def gemit(j, total):
        gram_ref[...] = total

    chain_sum(me, n, chunks, part, compute, emit, (send_r, send_l, recv_l, recv_r), ssem, rsem)
    chain_sum(me, n, 1, gpart, gcompute, gemit, (gsend_r, gsend_l, grecv_l, grecv_r), gssem, grsem)


def cross_call(n, deltas, y):
    rows, ff = deltas.shape
    rank = y.shape[1]
    tile = 256 if rows % 256 == 0 else 128
    chunks = ff // CHUNK
    comm = pltpu.VMEM((chunks, rank, CHUNK), BF16)
    gcomm = pltpu.VMEM((1, rank, rank), F32)
    vmem = pl.BlockSpec(memory_space=pltpu.VMEM)
    return pl.pallas_call(
        functools.partial(cross_kernel, n, tile, chunks),
        out_shape=(jax.ShapeDtypeStruct((rank, rank), F32), jax.ShapeDtypeStruct((rank, ff // n), F32)),
        in_specs=[vmem, vmem],
        out_specs=(vmem, vmem),
        scratch_shapes=[
            pltpu.VMEM((rank, rows), BF16),
            pltpu.VMEM((chunks, rank, CHUNK), F32),
            gcomm,
            gcomm, gcomm, gcomm, gcomm,
            comm, comm, comm, comm,
            pltpu.SemaphoreType.DMA((2, 1)),
            pltpu.SemaphoreType.DMA((2, 1)),
            pltpu.SemaphoreType.DMA((2, chunks)),
            pltpu.SemaphoreType.DMA((2, chunks)),
        ],
        compiler_params=pltpu.CompilerParams(
            collective_id=1, has_side_effects=True, vmem_limit_bytes=VMEM_LIMIT),
        cost_estimate=pl.CostEstimate(
            flops=2 * rows * ff * rank * 20, bytes_accessed=rows * ff * 2, transcendentals=0),
        name="cross_gram",
    )(deltas, y)


def mul(a, b):
    return jnp.dot(a, b, preferred_element_type=F32, precision=lax.Precision.HIGHEST)


def solve_kernel(gram_ref, cross_ref, out_ref, g_ref, x_ref):
    gram = gram_ref[...]
    rank = gram.shape[0]
    eye = lax.broadcasted_iota(jnp.int32, gram.shape, 0) == lax.broadcasted_iota(jnp.int32, gram.shape, 1)
    one = jnp.where(eye, F32(1), F32(0))
    diag = jnp.where(eye, gram, F32(0))
    down = lax.rsqrt(jnp.sum(diag, axis=1, keepdims=True))
    across = lax.rsqrt(jnp.sum(diag, axis=0, keepdims=True))
    g = gram * down * across
    g_ref[...] = g
    x_ref[...] = one / jnp.max(jnp.sum(jnp.abs(g), axis=1))

    def going(carry):
        count, left = carry
        return (count < 64) & (left > 1e-6)

    def newton(carry):
        count, _ = carry
        x = x_ref[...]
        miss = one - mul(g_ref[...], x)
        x_ref[...] = x + mul(x, miss)
        return count + 1, jnp.sum(miss * miss)

    lax.while_loop(going, newton, (jnp.int32(0), F32(1e9)))
    out_ref[...] = (mul(x_ref[...], cross_ref[...] * down) * down).astype(BF16)


def solve_call(gram, cross):
    vmem = pl.BlockSpec(memory_space=pltpu.VMEM)
    return pl.pallas_call(
        solve_kernel,
        out_shape=jax.ShapeDtypeStruct(cross.shape, BF16),
        in_specs=[vmem, vmem],
        out_specs=vmem,
        scratch_shapes=[pltpu.VMEM(gram.shape, F32), pltpu.VMEM(gram.shape, F32)],
        compiler_params=pltpu.CompilerParams(vmem_limit_bytes=VMEM_LIMIT),
        cost_estimate=pl.CostEstimate(flops=10 * 10**9, bytes_accessed=10**6, transcendentals=0),
        name="solve",
    )(gram, cross)


def update_kernel(chosen_ref, present_ref, y_ref, c_ref, serving_ref, out_ref):
    update = jnp.dot(y_ref[0], c_ref[0], preferred_element_type=F32)
    update = jnp.where(present_ref[pl.program_id(0)] == 1, update, F32(0))
    out_ref[0] = (serving_ref[0].astype(F32) + update).astype(BF16)


def update_call(chosen, present, ys, coeffs, serving):
    slots, rows, ff = serving.shape
    rank = ys.shape[2]
    tile = 256 if rows % 256 == 0 else 128
    return pl.pallas_call(
        update_kernel,
        out_shape=jax.ShapeDtypeStruct(serving.shape, BF16),
        grid_spec=pltpu.PrefetchScalarGridSpec(
            num_scalar_prefetch=2,
            grid=(slots, rows // tile),
            in_specs=[
                pl.BlockSpec((1, tile, rank), lambda s, i, c, p: (c[s], i, 0)),
                pl.BlockSpec((1, rank, ff), lambda s, i, c, p: (s, 0, 0)),
                pl.BlockSpec((1, tile, ff), lambda s, i, c, p: (s, i, 0)),
            ],
            out_specs=pl.BlockSpec((1, tile, ff), lambda s, i, c, p: (s, i, 0)),
        ),
        compiler_params=pltpu.CompilerParams(vmem_limit_bytes=VMEM_LIMIT),
        cost_estimate=pl.CostEstimate(
            flops=2 * slots * rows * ff * rank, bytes_accessed=4 * slots * rows * ff, transcendentals=0),
        name="update",
    )(chosen, present, ys, coeffs, serving)


def local(n, deltas, sketch_matrix, owner_of, serving):
    slot_count = serving.shape[0]
    own_index = lax.axis_index("ep")
    delta_rows = deltas[0]

    is_owned = (owner_of == own_index).astype(jnp.int32)
    owned_rank = jnp.cumsum(is_owned, dtype=jnp.int32) - 1
    slot_ids = jnp.arange(slot_count, dtype=jnp.int32)
    hits = (is_owned[None, :] == 1) & (owned_rank[None, :] == slot_ids[:, None])
    present = jnp.any(hits, axis=1).astype(jnp.int32)
    expert_ids = jnp.arange(owner_of.shape[0], dtype=jnp.int32)
    chosen = jnp.sum(jnp.where(hits, expert_ids[None, :], 0), axis=1).astype(jnp.int32)

    y = power_call(n, delta_rows, sketch_matrix)
    ys = lax.all_gather(y, "ep", axis=0)
    gram, cross = cross_call(n, delta_rows, y)
    coeffs = solve_call(gram, cross)
    coeff_stack = lax.all_gather(coeffs, "ep", axis=0)
    picked = jnp.stack([lax.dynamic_index_in_dim(coeff_stack, chosen[s], 0, keepdims=False) for s in range(slot_count)])
    full = lax.all_gather(picked, "fsdp", axis=2, tiled=True)
    return update_call(chosen, present, ys, full, serving)


def solution(mesh):
    return jax.shard_map(
        functools.partial(local, mesh.shape["fsdp"]),
        mesh=mesh,
        in_specs=(P("ep", "fsdp", None), P(), P(), P("ep", "fsdp", None)),
        out_specs=P("ep", "fsdp", None),
        check_vma=False,
    )
```

```python
import functools

import jax
import jax.numpy as jnp
from jax import lax
from jax.experimental import pallas as pl
from jax.experimental.pallas import tpu as pltpu
from jax.sharding import PartitionSpec as P

D = 7168
POWER = 2
MESH = pl.DeviceIdType.MESH
CHUNK = 256
VMEM_LIMIT = 56 * 1024 * 1024
F32 = jnp.float32
BF16 = jnp.bfloat16


def flip(me, bits):
    for bit in bits:
        me = me + (1 - 2 * lax.rem(lax.div(me, 1 << bit), 2)) * (1 << bit)
    return me


def digits(count):
    return list(range(count.bit_length() - 1))


def greet(me, n, own=None, bits=()):
    barrier = pltpu.get_barrier_semaphore()
    for bit in bits:
        pl.semaphore_signal(barrier, inc=1, device_id={"ep": flip(own, [bit])}, device_id_type=MESH)
    peers = len(bits)
    if n > 0:
        @pl.when(me > 0)
        def _():
            pl.semaphore_signal(barrier, inc=1, device_id={"fsdp": me - 1}, device_id_type=MESH)

        @pl.when(me < n - 1)
        def _():
            pl.semaphore_signal(barrier, inc=1, device_id={"fsdp": me + 1}, device_id_type=MESH)

        peers = peers + (me > 0).astype(jnp.int32) + (me < n - 1).astype(jnp.int32)
    pl.semaphore_wait(barrier, peers)


class Cube:
    def __init__(self, own, order, at, ssem, rsem):
        self.own, self.order, self.at, self.ssem, self.rsem = own, order, at, ssem, rsem

    def copy(self, held, bit, index):
        block = self.at(flip(self.own, held))
        return pltpu.make_async_remote_copy(
            src_ref=block, dst_ref=block, send_sem=self.ssem.at[index], recv_sem=self.rsem.at[index],
            device_id={"ep": flip(self.own, [bit])}, device_id_type=MESH)

    def held(self, stage):
        sets = [[]]
        for bit in self.order[:stage]:
            sets = sets + [one + [bit] for one in sets]
        return sets

    def across(self, stage):
        bit, base = self.order[stage], (1 << stage) - 1
        return [(one, bit, base + i) for i, one in enumerate(self.held(stage))]

    def beside(self, stage):
        base = (1 << len(self.order)) - 1
        sets = list(enumerate(self.held(stage)))
        first = 0 if stage == 0 else 1 << (stage - 1)
        return [(one, 0, base + i) for i, one in sets[first:]]

    def arrive(self, plans):
        for one, bit, index in plans:
            self.copy(one + [bit], bit, index).wait_recv()

    def run(self, stage):
        if stage > 0:
            self.arrive(self.across(stage - 1))
        if stage < len(self.order):
            for plan in self.across(stage):
                self.copy(*plan).start()
        for plan in self.beside(stage):
            self.copy(*plan).start()

    def finish(self):
        for stage in range(len(self.order) + 1):
            self.arrive(self.beside(stage))
            plans = self.beside(stage)
            if stage < len(self.order):
                plans = plans + self.across(stage)
            for plan in plans:
                self.copy(*plan).wait_send()


def cubes(own, count, ref, halves, ssem, rsem):
    inner = digits(count)[1:]
    half = ref.shape[1] // halves
    found = []
    for h in range(halves):
        order = inner if h % 2 == 0 else inner[::-1]
        found.append(Cube(own, order, lambda e, h=h: ref.at[e, pl.ds(h * half, half)], ssem.at[h], rsem.at[h]))
    return found


def moves(me, n, part, bufs, ssem, rsem):
    send_r, send_l, recv_l, recv_r = bufs
    def to_right(j):
        return pltpu.make_async_remote_copy(
            src_ref=send_r.at[j], dst_ref=recv_l.at[j], send_sem=ssem.at[0, j],
            recv_sem=rsem.at[0, j], device_id={"fsdp": jnp.minimum(me + 1, n - 1)}, device_id_type=MESH)

    def to_left(j):
        return pltpu.make_async_remote_copy(
            src_ref=send_l.at[j], dst_ref=recv_r.at[j], send_sem=ssem.at[1, j],
            recv_sem=rsem.at[1, j], device_id={"fsdp": jnp.maximum(me - 1, 0)}, device_id_type=MESH)

    @pl.when(me == 0)
    def _():
        recv_l[...] = jnp.zeros_like(recv_l)

    @pl.when(me == n - 1)
    def _():
        recv_r[...] = jnp.zeros_like(recv_r)

    def rightward(j):
        @pl.when(me > 0)
        def _():
            to_right(j).wait_recv()

        @pl.when(me < n - 1)
        def _():
            send_r[j] = (part[j] + recv_l[j].astype(F32)).astype(send_r.dtype)
            to_right(j).start()

    def leftward(j):
        @pl.when(me < n - 1)
        def _():
            to_left(j).wait_recv()

        @pl.when(me > 0)
        def _():
            send_l[j] = (part[j] + recv_r[j].astype(F32)).astype(send_l.dtype)
            to_left(j).start()

    def total(j):
        return part[j] + recv_l[j].astype(F32) + recv_r[j].astype(F32)

    def drain(j, carry):
        @pl.when(me < n - 1)
        def _():
            to_right(j).wait_send()

        @pl.when(me > 0)
        def _():
            to_left(j).wait_send()

        return carry

    return rightward, leftward, total, drain


def chain_sum(me, n, chunks, part, compute, emit, bufs, ssem, rsem, first=None):
    lower = me < n // 2
    edge = jnp.minimum(me, n - 1 - me)
    skew = jnp.where(edge == 0, chunks, jnp.minimum(n - 2 * edge, chunks))
    rightward, leftward, total, drain = moves(me, n, part, bufs, ssem, rsem)
    if first is not None:
        fpart, fcompute, femit, fbufs, fssem, frsem = first
        frightward, fleftward, ftotal, fdrain = moves(me, n, fpart, fbufs, fssem, frsem)

    def step(t, carry):
        if first is not None:
            @pl.when(t == 0)
            def _():
                fpart[0] = fcompute()

                @pl.when(lower)
                def _():
                    frightward(0)

                @pl.when(jnp.logical_not(lower))
                def _():
                    fleftward(0)

            @pl.when(t == skew)
            def _():
                @pl.when(lower)
                def _():
                    fleftward(0)

                @pl.when(jnp.logical_not(lower))
                def _():
                    frightward(0)

                femit(ftotal(0))

        @pl.when(t < chunks)
        def _():
            part[t] = compute(t)

            @pl.when(lower)
            def _():
                rightward(t)

            @pl.when(jnp.logical_not(lower))
            def _():
                leftward(t)

        @pl.when((t >= skew) & (t < skew + chunks))
        def _():
            j = t - skew

            @pl.when(lower)
            def _():
                leftward(j)

            @pl.when(jnp.logical_not(lower))
            def _():
                rightward(j)

            emit(j, total(j))

        return carry

    lax.fori_loop(0, 2 * chunks, step, 0)

    lax.fori_loop(0, chunks, drain, 0)
    if first is not None:
        fdrain(0, 0)


def power_kernel(n, tile, chunks, a_ref, w_ref, y_ref, yt, p, part, send_r, send_l, recv_l, recv_r, ssem, rsem):
    me = lax.axis_index("fsdp")
    rows = a_ref.shape[0]
    greet(me, n)

    def sketch(weights):
        def body(i, carry):
            at = pl.ds(pl.multiple_of(i * tile, tile), tile)
            block = jnp.dot(a_ref[at, :], weights[...], preferred_element_type=F32)
            y_ref[at, :] = block.astype(BF16)
            yt[:, at] = block.T.astype(BF16)
            return carry

        lax.fori_loop(0, rows // tile, body, 0)

    def compute(j):
        at = pl.ds(pl.multiple_of(j * CHUNK, CHUNK), CHUNK)
        return jnp.dot(yt[...], a_ref[:, at], preferred_element_type=F32)

    def emit(j, total):
        at = pl.ds(pl.multiple_of(j * CHUNK, CHUNK), CHUNK)
        p[at, :] = (total / D).T.astype(BF16)

    sketch(w_ref)
    for i in range(POWER):
        bufs = [b.at[i] for b in (send_r, send_l, recv_l, recv_r)]
        chain_sum(me, n, chunks, part, compute, emit, bufs, ssem.at[i], rsem.at[i])
        sketch(p)


def power_call(n, deltas, weights):
    rows, ff = deltas.shape
    rank = weights.shape[1]
    tile = 256 if rows % 256 == 0 else 128
    chunks = ff // CHUNK
    comm = pltpu.VMEM((POWER, chunks, rank, CHUNK), BF16)
    vmem = pl.BlockSpec(memory_space=pltpu.VMEM)
    return pl.pallas_call(
        functools.partial(power_kernel, n, tile, chunks),
        out_shape=jax.ShapeDtypeStruct((rows, rank), BF16),
        in_specs=[vmem, vmem],
        out_specs=vmem,
        scratch_shapes=[
            pltpu.VMEM((rank, rows), BF16),
            pltpu.VMEM((ff, rank), BF16),
            pltpu.VMEM((chunks, rank, CHUNK), F32),
            comm, comm, comm, comm,
            pltpu.SemaphoreType.DMA((POWER, 2, chunks)),
            pltpu.SemaphoreType.DMA((POWER, 2, chunks)),
        ],
        compiler_params=pltpu.CompilerParams(
            collective_id=0, has_side_effects=True, vmem_limit_bytes=VMEM_LIMIT),
        cost_estimate=pl.CostEstimate(
            flops=2 * rows * ff * rank * 5, bytes_accessed=rows * ff * 2, transcendentals=0),
        name="power_steps",
    )(deltas, weights)


def cross_kernel(n, count, tile, chunks, a_ref, y_ref, gram_ref, cross_ref, ys_ref, yt, part, gpart,
                 gsend_r, gsend_l, grecv_l, grecv_r, send_r, send_l, recv_l, recv_r,
                 gssem, grsem, ssem, rsem, cssem, crsem, own_sem):
    me, own = lax.axis_index("fsdp"), lax.axis_index("ep")
    rows = a_ref.shape[0]
    bits = digits(count)
    greet(me, n, own, bits)

    place = pltpu.make_async_copy(y_ref, ys_ref.at[own], own_sem)
    place.start()
    place.wait()
    gathers = cubes(own, count, ys_ref, 2, cssem, crsem)
    stages = len(bits) - 1
    for gather in gathers:
        gather.run(0)

    def turn(i, carry):
        at = pl.ds(pl.multiple_of(i * tile, tile), tile)
        yt[:, at] = y_ref[at, :].astype(F32).T.astype(BF16)
        return carry

    lax.fori_loop(0, rows // tile, turn, 0)

    def compute(j):
        at = pl.ds(pl.multiple_of(j * CHUNK, CHUNK), CHUNK)
        return jnp.dot(yt[...], a_ref[:, at], preferred_element_type=F32)

    def emit(j, total):
        at = pl.ds(pl.multiple_of(j * CHUNK, CHUNK), CHUNK)
        cross_ref[:, at] = total

        @pl.when(j == chunks // 2 - 1)
        def _():
            for gather in gathers:
                gather.run(1)

    def gcompute():
        return jnp.dot(yt[...], y_ref[...], preferred_element_type=F32)

    def gemit(total):
        gram_ref[...] = total

    chain_sum(me, n, chunks, part, compute, emit, (send_r, send_l, recv_l, recv_r), ssem, rsem,
              (gpart, gcompute, gemit, (gsend_r, gsend_l, grecv_l, grecv_r), gssem, grsem))
    for stage in range(2, stages + 1):
        for gather in gathers:
            gather.run(stage)
    for gather in gathers:
        gather.finish()


def cross_call(n, count, deltas, y):
    rows, ff = deltas.shape
    rank = y.shape[1]
    tile = 256 if rows % 256 == 0 else 128
    chunks = ff // CHUNK
    comm = pltpu.VMEM((chunks, rank, CHUNK), BF16)
    gcomm = pltpu.VMEM((1, rank, rank), F32)
    vmem = pl.BlockSpec(memory_space=pltpu.VMEM)
    return pl.pallas_call(
        functools.partial(cross_kernel, n, count, tile, chunks),
        out_shape=(
            jax.ShapeDtypeStruct((rank, rank), F32),
            jax.ShapeDtypeStruct((rank, ff), F32),
            jax.ShapeDtypeStruct((count, rows, rank), BF16),
        ),
        in_specs=[vmem, vmem],
        out_specs=(vmem, vmem, pl.BlockSpec(memory_space=pl.ANY)),
        scratch_shapes=[
            pltpu.VMEM((rank, rows), BF16),
            pltpu.VMEM((chunks, rank, CHUNK), F32),
            gcomm,
            gcomm, gcomm, gcomm, gcomm,
            comm, comm, comm, comm,
            pltpu.SemaphoreType.DMA((2, 1)),
            pltpu.SemaphoreType.DMA((2, 1)),
            pltpu.SemaphoreType.DMA((2, chunks)),
            pltpu.SemaphoreType.DMA((2, chunks)),
            pltpu.SemaphoreType.DMA((2, count - 1)),
            pltpu.SemaphoreType.DMA((2, count - 1)),
            pltpu.SemaphoreType.DMA,
        ],
        compiler_params=pltpu.CompilerParams(
            collective_id=1, has_side_effects=True, vmem_limit_bytes=VMEM_LIMIT),
        cost_estimate=pl.CostEstimate(
            flops=2 * rows * ff * rank * 20, bytes_accessed=rows * ff * 2, transcendentals=0),
        name="cross_gram",
    )(deltas, y)


def share_kernel(count, block_ref, out_ref, ssem, rsem, own_sem):
    own = lax.axis_index("ep")
    bits = digits(count)
    greet(0, 0, own, bits)
    place = pltpu.make_async_copy(block_ref, out_ref.at[own], own_sem)
    place.start()
    place.wait()
    gathers = cubes(own, count, out_ref, 2, ssem, rsem)
    for stage in range(len(bits)):
        for gather in gathers:
            gather.run(stage)
    for gather in gathers:
        gather.finish()


def share_call(count, block):
    return pl.pallas_call(
        functools.partial(share_kernel, count),
        out_shape=jax.ShapeDtypeStruct((count,) + block.shape, block.dtype),
        in_specs=[pl.BlockSpec(memory_space=pl.ANY)],
        out_specs=pl.BlockSpec(memory_space=pl.ANY),
        scratch_shapes=[
            pltpu.SemaphoreType.DMA((2, count - 1)),
            pltpu.SemaphoreType.DMA((2, count - 1)),
            pltpu.SemaphoreType.DMA,
        ],
        compiler_params=pltpu.CompilerParams(
            collective_id=2, has_side_effects=True, vmem_limit_bytes=VMEM_LIMIT),
        name="share_coeffs",
    )(block)


def mul(a, b):
    return jnp.dot(a, b, preferred_element_type=F32, precision=lax.Precision.HIGHEST)


def solve_kernel(gram_ref, cross_ref, out_ref, g_ref, x_ref):
    gram = gram_ref[...]
    rank = gram.shape[0]
    eye = lax.broadcasted_iota(jnp.int32, gram.shape, 0) == lax.broadcasted_iota(jnp.int32, gram.shape, 1)
    one = jnp.where(eye, F32(1), F32(0))
    diag = jnp.where(eye, gram, F32(0))
    down = lax.rsqrt(jnp.sum(diag, axis=1, keepdims=True))
    across = lax.rsqrt(jnp.sum(diag, axis=0, keepdims=True))
    g = gram * down * across
    g_ref[...] = g
    x_ref[...] = one / jnp.max(jnp.sum(jnp.abs(g), axis=1))

    def going(carry):
        count, left = carry
        return (count < 64) & (left > 1e-6)

    def newton(carry):
        count, _ = carry
        x = x_ref[...]
        miss = one - mul(g_ref[...], x)
        x_ref[...] = x + mul(x, miss)
        return count + 1, jnp.sum(miss * miss)

    lax.while_loop(going, newton, (jnp.int32(0), F32(1e9)))
    out_ref[...] = (mul(x_ref[...], cross_ref[...] * down) * down).astype(BF16)


def solve_call(gram, cross):
    vmem = pl.BlockSpec(memory_space=pltpu.VMEM)
    return pl.pallas_call(
        solve_kernel,
        out_shape=jax.ShapeDtypeStruct(cross.shape, BF16),
        in_specs=[vmem, vmem],
        out_specs=vmem,
        scratch_shapes=[pltpu.VMEM(gram.shape, F32), pltpu.VMEM(gram.shape, F32)],
        compiler_params=pltpu.CompilerParams(vmem_limit_bytes=VMEM_LIMIT),
        cost_estimate=pl.CostEstimate(flops=10 * 10**9, bytes_accessed=10**6, transcendentals=0),
        name="solve",
    )(gram, cross)


def update_kernel(chosen_ref, present_ref, y_ref, c_ref, serving_ref, out_ref):
    y = jnp.where(present_ref[pl.program_id(0)] == 1, y_ref[0].astype(F32), F32(0)).astype(BF16)
    update = jnp.dot(y, c_ref[0], preferred_element_type=F32)
    out_ref[0] = (serving_ref[0].astype(F32) + update).astype(BF16)


def update_call(chosen, present, ys, coeffs, serving):
    slots, rows, ff = serving.shape
    rank = ys.shape[2]
    tile = rows // 4
    return pl.pallas_call(
        update_kernel,
        out_shape=jax.ShapeDtypeStruct(serving.shape, BF16),
        grid_spec=pltpu.PrefetchScalarGridSpec(
            num_scalar_prefetch=2,
            grid=(slots, rows // tile),
            in_specs=[
                pl.BlockSpec((1, tile, rank), lambda s, i, c, p: (c[s], i, 0)),
                pl.BlockSpec((1, rank, ff), lambda s, i, c, p: (c[s], 0, 0)),
                pl.BlockSpec((1, tile, ff), lambda s, i, c, p: (s, i, 0)),
            ],
            out_specs=pl.BlockSpec((1, tile, ff), lambda s, i, c, p: (s, i, 0)),
        ),
        compiler_params=pltpu.CompilerParams(vmem_limit_bytes=VMEM_LIMIT),
        cost_estimate=pl.CostEstimate(
            flops=2 * slots * rows * ff * rank, bytes_accessed=4 * slots * rows * ff, transcendentals=0),
        name="update",
    )(chosen, present, ys, coeffs, serving)


def local(n, count, deltas, sketch_matrix, owner_of, serving):
    slot_count = serving.shape[0]
    own_index = lax.axis_index("ep")
    delta_rows = deltas[0]

    is_owned = (owner_of == own_index).astype(jnp.int32)
    owned_rank = jnp.cumsum(is_owned, dtype=jnp.int32) - 1
    slot_ids = jnp.arange(slot_count, dtype=jnp.int32)
    hits = (is_owned[None, :] == 1) & (owned_rank[None, :] == slot_ids[:, None])
    present = jnp.any(hits, axis=1).astype(jnp.int32)
    expert_ids = jnp.arange(owner_of.shape[0], dtype=jnp.int32)
    chosen = jnp.sum(jnp.where(hits, expert_ids[None, :], 0), axis=1).astype(jnp.int32)

    y = power_call(n, delta_rows, sketch_matrix)
    gram, cross, ys = cross_call(n, count, delta_rows, y)
    coeffs = share_call(count, solve_call(gram, cross))
    return update_call(chosen, present, ys, coeffs, serving)


def solution(mesh):
    return jax.shard_map(
        functools.partial(local, mesh.shape["fsdp"], mesh.shape["ep"]),
        mesh=mesh,
        in_specs=(P("ep", "fsdp", None), P(), P(), P("ep", "fsdp", None)),
        out_specs=P("ep", "fsdp", None),
        check_vma=False,
    )
```

```python
import functools

import jax
import jax.numpy as jnp
from jax import lax
from jax.experimental import pallas as pl
from jax.experimental.pallas import tpu as pltpu
from jax.sharding import PartitionSpec as P

D = 7168
POWER = 2
MESH = pl.DeviceIdType.MESH
CHUNK = 128
VMEM_LIMIT = 56 * 1024 * 1024
F32 = jnp.float32
BF16 = jnp.bfloat16


def flip(me, bits):
    for bit in bits:
        me = me + (1 - 2 * lax.rem(lax.div(me, 1 << bit), 2)) * (1 << bit)
    return me


def digits(count):
    return list(range(count.bit_length() - 1))


def greet(me, n, own=None, bits=()):
    barrier = pltpu.get_barrier_semaphore()
    for bit in bits:
        pl.semaphore_signal(barrier, inc=1, device_id={"ep": flip(own, [bit])}, device_id_type=MESH)
    peers = len(bits)
    if n > 0:
        @pl.when(me > 0)
        def _():
            pl.semaphore_signal(barrier, inc=1, device_id={"fsdp": me - 1}, device_id_type=MESH)

        @pl.when(me < n - 1)
        def _():
            pl.semaphore_signal(barrier, inc=1, device_id={"fsdp": me + 1}, device_id_type=MESH)

        peers = peers + (me > 0).astype(jnp.int32) + (me < n - 1).astype(jnp.int32)
    pl.semaphore_wait(barrier, peers)


class Cube:
    def __init__(self, own, order, at, ssem, rsem):
        self.own, self.order, self.at, self.ssem, self.rsem = own, order, at, ssem, rsem

    def copy(self, held, bit, index):
        block = self.at(lax.div(flip(self.own, held), 2))
        return pltpu.make_async_remote_copy(
            src_ref=block, dst_ref=block, send_sem=self.ssem.at[index], recv_sem=self.rsem.at[index],
            device_id={"ep": flip(self.own, [bit])}, device_id_type=MESH)

    def across(self, stage):
        sets = [[]]
        for bit in self.order[:stage]:
            sets = sets + [one + [bit] for one in sets]
        return [(one, self.order[stage], (1 << stage) - 1 + i) for i, one in enumerate(sets)]

    def run(self, stage):
        if stage > 0:
            for one, bit, index in self.across(stage - 1):
                self.copy(one + [bit], bit, index).wait_recv()
        if stage < len(self.order):
            for plan in self.across(stage):
                self.copy(*plan).start()

    def finish(self):
        for stage in range(len(self.order)):
            for plan in self.across(stage):
                self.copy(*plan).wait_send()


def cubes(own, count, ref, ssem, rsem):
    inner = digits(count)[1:]
    half = ref.shape[1] // 2
    return [
        Cube(own, order, lambda e, h=h: ref.at[e, pl.ds(h * half, half)], ssem.at[h], rsem.at[h])
        for h, order in enumerate((inner, inner[::-1]))
    ]


def moves(me, n, part, bufs, ssem, rsem):
    send_r, send_l, recv_l, recv_r = bufs
    def to_right(j):
        return pltpu.make_async_remote_copy(
            src_ref=send_r.at[j], dst_ref=recv_l.at[j], send_sem=ssem.at[0, j],
            recv_sem=rsem.at[0, j], device_id={"fsdp": jnp.minimum(me + 1, n - 1)}, device_id_type=MESH)

    def to_left(j):
        return pltpu.make_async_remote_copy(
            src_ref=send_l.at[j], dst_ref=recv_r.at[j], send_sem=ssem.at[1, j],
            recv_sem=rsem.at[1, j], device_id={"fsdp": jnp.maximum(me - 1, 0)}, device_id_type=MESH)

    @pl.when(me == 0)
    def _():
        recv_l[...] = jnp.zeros_like(recv_l)

    @pl.when(me == n - 1)
    def _():
        recv_r[...] = jnp.zeros_like(recv_r)

    def rightward(j):
        @pl.when(me > 0)
        def _():
            to_right(j).wait_recv()

        @pl.when(me < n - 1)
        def _():
            send_r[j] = (part[j] + recv_l[j].astype(F32)).astype(send_r.dtype)
            to_right(j).start()

    def leftward(j):
        @pl.when(me < n - 1)
        def _():
            to_left(j).wait_recv()

        @pl.when(me > 0)
        def _():
            send_l[j] = (part[j] + recv_r[j].astype(F32)).astype(send_l.dtype)
            to_left(j).start()

    def total(j):
        return part[j] + recv_l[j].astype(F32) + recv_r[j].astype(F32)

    def drain(j, carry):
        @pl.when(me < n - 1)
        def _():
            to_right(j).wait_send()

        @pl.when(me > 0)
        def _():
            to_left(j).wait_send()

        return carry

    return rightward, leftward, total, drain


def chain_sum(me, n, chunks, part, compute, emit, bufs, ssem, rsem, first=None):
    lower = me < n // 2
    edge = jnp.minimum(me, n - 1 - me)
    skew = jnp.where(edge == 0, chunks, jnp.minimum(n - 2 * edge, chunks))
    rightward, leftward, total, drain = moves(me, n, part, bufs, ssem, rsem)
    if first is not None:
        fpart, fcompute, femit, fbufs, fssem, frsem = first
        frightward, fleftward, ftotal, fdrain = moves(me, n, fpart, fbufs, fssem, frsem)

    def step(t, carry):
        if first is not None:
            @pl.when(t == 0)
            def _():
                fpart[0] = fcompute()

                @pl.when(lower)
                def _():
                    frightward(0)

                @pl.when(jnp.logical_not(lower))
                def _():
                    fleftward(0)

            @pl.when(t == skew)
            def _():
                @pl.when(lower)
                def _():
                    fleftward(0)

                @pl.when(jnp.logical_not(lower))
                def _():
                    frightward(0)

                femit(ftotal(0))

        @pl.when(t < chunks)
        def _():
            part[t] = compute(t)

            @pl.when(lower)
            def _():
                rightward(t)

            @pl.when(jnp.logical_not(lower))
            def _():
                leftward(t)

        @pl.when((t >= skew) & (t < skew + chunks))
        def _():
            j = t - skew

            @pl.when(lower)
            def _():
                leftward(j)

            @pl.when(jnp.logical_not(lower))
            def _():
                rightward(j)

            emit(j, total(j))

        return carry

    lax.fori_loop(0, 2 * chunks, step, 0)

    lax.fori_loop(0, chunks, drain, 0)
    if first is not None:
        fdrain(0, 0)


def power_kernel(n, tile, chunks, a_ref, w_ref, y_ref, yt, p, part, send_r, send_l, recv_l, recv_r, ssem, rsem):
    me = lax.axis_index("fsdp")
    rows = a_ref.shape[0]
    greet(me, n)

    def sketch(weights):
        def body(i, carry):
            at = pl.ds(pl.multiple_of(i * tile, tile), tile)
            block = jnp.dot(a_ref[at, :], weights[...], preferred_element_type=F32)
            y_ref[at, :] = block.astype(BF16)
            yt[:, at] = block.T.astype(BF16)
            return carry

        lax.fori_loop(0, rows // tile, body, 0)

    def compute(j):
        at = pl.ds(pl.multiple_of(j * CHUNK, CHUNK), CHUNK)
        return jnp.dot(yt[...], a_ref[:, at], preferred_element_type=F32)

    def emit(j, total):
        at = pl.ds(pl.multiple_of(j * CHUNK, CHUNK), CHUNK)
        p[at, :] = (total / D).T.astype(BF16)

    sketch(w_ref)
    for i in range(POWER):
        bufs = [b.at[i] for b in (send_r, send_l, recv_l, recv_r)]
        chain_sum(me, n, chunks, part, compute, emit, bufs, ssem.at[i], rsem.at[i])
        sketch(p)


def power_call(n, deltas, weights):
    rows, ff = deltas.shape
    rank = weights.shape[1]
    tile = 256 if rows % 256 == 0 else 128
    chunks = ff // CHUNK
    comm = pltpu.VMEM((POWER, chunks, rank, CHUNK), BF16)
    vmem = pl.BlockSpec(memory_space=pltpu.VMEM)
    return pl.pallas_call(
        functools.partial(power_kernel, n, tile, chunks),
        out_shape=jax.ShapeDtypeStruct((rows, rank), BF16),
        in_specs=[vmem, vmem],
        out_specs=vmem,
        scratch_shapes=[
            pltpu.VMEM((rank, rows), BF16),
            pltpu.VMEM((ff, rank), BF16),
            pltpu.VMEM((chunks, rank, CHUNK), F32),
            comm, comm, comm, comm,
            pltpu.SemaphoreType.DMA((POWER, 2, chunks)),
            pltpu.SemaphoreType.DMA((POWER, 2, chunks)),
        ],
        compiler_params=pltpu.CompilerParams(
            collective_id=0, has_side_effects=True, vmem_limit_bytes=VMEM_LIMIT),
        cost_estimate=pl.CostEstimate(
            flops=2 * rows * ff * rank * 5, bytes_accessed=rows * ff * 2, transcendentals=0),
        name="power_steps",
    )(deltas, weights)


def cross_kernel(n, count, tile, chunks, a_ref, y_ref, gram_ref, cross_ref, ys_ref, yt, part, gpart,
                 gsend_r, gsend_l, grecv_l, grecv_r, send_r, send_l, recv_l, recv_r,
                 gssem, grsem, ssem, rsem, cssem, crsem, own_sem):
    me, own = lax.axis_index("fsdp"), lax.axis_index("ep")
    rows = a_ref.shape[0]
    bits = digits(count)
    greet(me, n, own, bits)

    place = pltpu.make_async_copy(y_ref, ys_ref.at[lax.div(own, 2)], own_sem)
    place.start()
    place.wait()
    gathers = cubes(own, count, ys_ref, cssem, crsem)
    stages = len(bits) - 1
    for gather in gathers:
        gather.run(0)

    def turn(i, carry):
        at = pl.ds(pl.multiple_of(i * tile, tile), tile)
        yt[:, at] = y_ref[at, :].astype(F32).T.astype(BF16)
        return carry

    lax.fori_loop(0, rows // tile, turn, 0)

    def compute(j):
        at = pl.ds(pl.multiple_of(j * CHUNK, CHUNK), CHUNK)
        return jnp.dot(yt[...], a_ref[:, at], preferred_element_type=F32)

    def emit(j, total):
        at = pl.ds(pl.multiple_of(j * CHUNK, CHUNK), CHUNK)
        cross_ref[:, at] = total

        @pl.when(j == chunks // 2 - 1)
        def _():
            for gather in gathers:
                gather.run(1)

    def gcompute():
        return jnp.dot(yt[...], y_ref[...], preferred_element_type=F32)

    def gemit(total):
        gram_ref[...] = total

    chain_sum(me, n, chunks, part, compute, emit, (send_r, send_l, recv_l, recv_r), ssem, rsem,
              (gpart, gcompute, gemit, (gsend_r, gsend_l, grecv_l, grecv_r), gssem, grsem))
    for stage in range(2, stages + 1):
        for gather in gathers:
            gather.run(stage)
    for gather in gathers:
        gather.finish()


def cross_call(n, count, deltas, y):
    rows, ff = deltas.shape
    rank = y.shape[1]
    tile = 256 if rows % 256 == 0 else 128
    chunks = ff // CHUNK
    comm = pltpu.VMEM((chunks, rank, CHUNK), BF16)
    gcomm = pltpu.VMEM((1, rank, rank), F32)
    vmem = pl.BlockSpec(memory_space=pltpu.VMEM)
    return pl.pallas_call(
        functools.partial(cross_kernel, n, count, tile, chunks),
        out_shape=(
            jax.ShapeDtypeStruct((rank, rank), F32),
            jax.ShapeDtypeStruct((rank, ff), F32),
            jax.ShapeDtypeStruct((count // 2, rows, rank), BF16),
        ),
        in_specs=[vmem, vmem],
        out_specs=(vmem, vmem, pl.BlockSpec(memory_space=pl.ANY)),
        scratch_shapes=[
            pltpu.VMEM((rank, rows), BF16),
            pltpu.VMEM((chunks, rank, CHUNK), F32),
            gcomm,
            gcomm, gcomm, gcomm, gcomm,
            comm, comm, comm, comm,
            pltpu.SemaphoreType.DMA((2, 1)),
            pltpu.SemaphoreType.DMA((2, 1)),
            pltpu.SemaphoreType.DMA((2, chunks)),
            pltpu.SemaphoreType.DMA((2, chunks)),
            pltpu.SemaphoreType.DMA((2, count // 2 - 1)),
            pltpu.SemaphoreType.DMA((2, count // 2 - 1)),
            pltpu.SemaphoreType.DMA,
        ],
        compiler_params=pltpu.CompilerParams(
            collective_id=1, has_side_effects=True, vmem_limit_bytes=VMEM_LIMIT),
        cost_estimate=pl.CostEstimate(
            flops=2 * rows * ff * rank * 20, bytes_accessed=rows * ff * 2, transcendentals=0),
        name="cross_gram",
    )(deltas, y)


def share_kernel(n, count, chosen_ref, other_ref, c_ref, yb_ref, c_out, y_out,
                 whole, piece, whole_send, whole_recv, piece_send, piece_recv, rows_z, y_send, y_recv,
                 wssem, wrsem, pssem, prsem, zssem, zrsem, bssem, brsem):
    me, own = lax.axis_index("fsdp"), lax.axis_index("ep")
    parity = lax.rem(own, 2)
    slots, rank, ff = c_out.shape
    half = ff // 2
    width = half // n
    bits = digits(count)
    stages = len(bits) - 1
    greet(me, n, own, bits)

    def beside(src, dst, index):
        return pltpu.make_async_remote_copy(
            src_ref=src, dst_ref=dst, send_sem=bssem.at[index], recv_sem=brsem.at[index],
            device_id={"ep": flip(own, [0])}, device_id_type=MESH)

    def for_partner(held, send):
        for s in range(slots):
            send[s] = held[lax.div(other_ref[s], 2)]

    def mine(held, recv, s):
        return jnp.where(lax.rem(chosen_ref[s], 2) == parity, held[lax.div(chosen_ref[s], 2)], recv[s])

    whole[lax.div(own, 2)] = c_ref[:, :half]
    piece[lax.div(own, 2)] = c_ref[:, pl.ds(pl.multiple_of(half + me * width, width), width)]
    pieces = cubes(own, count, piece, pssem, prsem)
    wholes = cubes(own, count, whole, wssem, wrsem)
    for gather in pieces + wholes:
        gather.run(0)
    for_partner(yb_ref, y_send)
    y_copy = beside(y_send, y_recv, 0)
    y_copy.start()
    for stage in range(1, stages):
        for gather in pieces + wholes:
            gather.run(stage)
    for gather in pieces:
        gather.run(stages)
    for_partner(piece, piece_send)
    piece_copy = beside(piece_send, piece_recv, 1)
    piece_copy.start()
    piece_copy.wait_recv()
    for s in range(slots):
        rows_z[me, s] = mine(piece, piece_recv, s)

    def right(block, hop):
        return pltpu.make_async_remote_copy(
            src_ref=rows_z.at[block], dst_ref=rows_z.at[block], send_sem=zssem.at[0, hop], recv_sem=zrsem.at[0, hop],
            device_id={"fsdp": jnp.minimum(me + 1, n - 1)}, device_id_type=MESH)

    def left(block, hop):
        return pltpu.make_async_remote_copy(
            src_ref=rows_z.at[block], dst_ref=rows_z.at[block], send_sem=zssem.at[1, hop], recv_sem=zrsem.at[1, hop],
            device_id={"fsdp": jnp.maximum(me - 1, 0)}, device_id_type=MESH)

    def send(hop, act):
        @pl.when((me - hop >= 0) & (me < n - 1))
        def _():
            act(right(me - hop, hop))

        @pl.when((me + hop <= n - 1) & (me > 0))
        def _():
            act(left(me + hop, hop))

    def receive(hop):
        @pl.when(me - 1 - hop >= 0)
        def _():
            right(me - 1 - hop, hop).wait_recv()

        @pl.when(me + 1 + hop <= n - 1)
        def _():
            left(me + 1 + hop, hop).wait_recv()

    send(0, lambda copy: copy.start())
    whole_copy = beside(whole_send, whole_recv, 2)
    for hop in range(n - 1):
        receive(hop)
        if hop < n - 2:
            send(hop + 1, lambda copy: copy.start())
        if hop == 0:
            for gather in wholes:
                gather.run(stages)
            for_partner(whole, whole_send)
            whole_copy.start()
    y_copy.wait_recv()
    for s in range(slots):
        y_out[s] = mine(yb_ref, y_recv, s)
    whole_copy.wait_recv()
    for s in range(slots):
        c_out[s, :, :half] = mine(whole, whole_recv, s)
        for z in range(n):
            c_out[s, :, half + z * width:half + (z + 1) * width] = rows_z[z, s]
    for gather in pieces + wholes:
        gather.finish()
    for copy in (y_copy, piece_copy, whole_copy):
        copy.wait_send()
    for hop in range(n - 1):
        send(hop, lambda copy: copy.wait_send())


def share_call(n, count, chosen, other, coeffs, held):
    rank, ff = coeffs.shape
    rows = held.shape[1]
    slots = chosen.shape[0]
    half, width = ff // 2, ff // 2 // n
    vmem = pl.BlockSpec(memory_space=pltpu.VMEM)
    smem = pl.BlockSpec(memory_space=pltpu.SMEM)
    dma = pltpu.SemaphoreType.DMA
    return pl.pallas_call(
        functools.partial(share_kernel, n, count),
        out_shape=(
            jax.ShapeDtypeStruct((slots, rank, ff), BF16),
            jax.ShapeDtypeStruct((slots, rows, rank), BF16),
        ),
        in_specs=[smem, smem, vmem, vmem],
        out_specs=(vmem, vmem),
        scratch_shapes=[
            pltpu.VMEM((count // 2, rank, half), BF16),
            pltpu.VMEM((count // 2, rank, width), BF16),
            pltpu.VMEM((slots, rank, half), BF16),
            pltpu.VMEM((slots, rank, half), BF16),
            pltpu.VMEM((slots, rank, width), BF16),
            pltpu.VMEM((slots, rank, width), BF16),
            pltpu.VMEM((n, slots, rank, width), BF16),
            pltpu.VMEM((slots, rows, rank), BF16),
            pltpu.VMEM((slots, rows, rank), BF16),
            dma((2, count // 2 - 1)), dma((2, count // 2 - 1)),
            dma((2, count // 2 - 1)), dma((2, count // 2 - 1)),
            dma((2, n - 1)), dma((2, n - 1)),
            dma((3,)), dma((3,)),
        ],
        compiler_params=pltpu.CompilerParams(
            collective_id=2, has_side_effects=True, vmem_limit_bytes=VMEM_LIMIT),
        name="share_chosen",
    )(chosen, other, coeffs, held)


def mul(a, b):
    return jnp.dot(a, b, preferred_element_type=F32, precision=lax.Precision.HIGHEST)


def solve_kernel(gram_ref, cross_ref, out_ref, g_ref, x_ref):
    gram = gram_ref[...]
    rank = gram.shape[0]
    eye = lax.broadcasted_iota(jnp.int32, gram.shape, 0) == lax.broadcasted_iota(jnp.int32, gram.shape, 1)
    one = jnp.where(eye, F32(1), F32(0))
    diag = jnp.where(eye, gram, F32(0))
    down = lax.rsqrt(jnp.sum(diag, axis=1, keepdims=True))
    across = lax.rsqrt(jnp.sum(diag, axis=0, keepdims=True))
    g = gram * down * across
    g_ref[...] = g
    x_ref[...] = one / jnp.max(jnp.sum(jnp.abs(g), axis=1))

    def going(carry):
        count, left = carry
        return (count < 64) & (left > 1e-6)

    def newton(carry):
        count, _ = carry
        x = x_ref[...]
        miss = one - mul(g_ref[...], x)
        x_ref[...] = x + mul(x, miss)
        return count + 1, jnp.sum(miss * miss)

    lax.while_loop(going, newton, (jnp.int32(0), F32(1e9)))
    out_ref[...] = (mul(x_ref[...], cross_ref[...] * down) * down).astype(BF16)


def solve_call(gram, cross):
    vmem = pl.BlockSpec(memory_space=pltpu.VMEM)
    return pl.pallas_call(
        solve_kernel,
        out_shape=jax.ShapeDtypeStruct(cross.shape, BF16),
        in_specs=[vmem, vmem],
        out_specs=vmem,
        scratch_shapes=[pltpu.VMEM(gram.shape, F32), pltpu.VMEM(gram.shape, F32)],
        compiler_params=pltpu.CompilerParams(vmem_limit_bytes=VMEM_LIMIT),
        cost_estimate=pl.CostEstimate(flops=10 * 10**9, bytes_accessed=10**6, transcendentals=0),
        name="solve",
    )(gram, cross)


def update_kernel(present_ref, y_ref, c_ref, serving_ref, out_ref):
    y = jnp.where(present_ref[pl.program_id(0)] == 1, y_ref[0].astype(F32), F32(0)).astype(BF16)
    update = jnp.dot(y, c_ref[0], preferred_element_type=F32)
    out_ref[0] = (serving_ref[0].astype(F32) + update).astype(BF16)


def update_call(present, ys, coeffs, serving):
    slots, rows, ff = serving.shape
    rank = ys.shape[2]
    tile = rows // 4
    return pl.pallas_call(
        update_kernel,
        out_shape=jax.ShapeDtypeStruct(serving.shape, BF16),
        grid_spec=pltpu.PrefetchScalarGridSpec(
            num_scalar_prefetch=1,
            grid=(slots, rows // tile),
            in_specs=[
                pl.BlockSpec((1, tile, rank), lambda s, i, p: (s, i, 0)),
                pl.BlockSpec((1, rank, ff), lambda s, i, p: (s, 0, 0)),
                pl.BlockSpec((1, tile, ff), lambda s, i, p: (s, i, 0)),
            ],
            out_specs=pl.BlockSpec((1, tile, ff), lambda s, i, p: (s, i, 0)),
        ),
        compiler_params=pltpu.CompilerParams(vmem_limit_bytes=VMEM_LIMIT),
        cost_estimate=pl.CostEstimate(
            flops=2 * slots * rows * ff * rank, bytes_accessed=4 * slots * rows * ff, transcendentals=0),
        name="update",
    )(present, ys, coeffs, serving)


def local(n, count, deltas, sketch_matrix, owner_of, serving):
    slot_count = serving.shape[0]
    own_index = lax.axis_index("ep")
    delta_rows = deltas[0]

    def slots_of(owner):
        is_owned = (owner_of == owner).astype(jnp.int32)
        owned_rank = jnp.cumsum(is_owned, dtype=jnp.int32) - 1
        slot_ids = jnp.arange(slot_count, dtype=jnp.int32)
        hits = (is_owned[None, :] == 1) & (owned_rank[None, :] == slot_ids[:, None])
        expert_ids = jnp.arange(owner_of.shape[0], dtype=jnp.int32)
        chosen = jnp.sum(jnp.where(hits, expert_ids[None, :], 0), axis=1).astype(jnp.int32)
        return chosen, jnp.any(hits, axis=1).astype(jnp.int32)

    chosen, present = slots_of(own_index)
    other, _ = slots_of(flip(own_index, [0]))

    y = power_call(n, delta_rows, sketch_matrix)
    gram, cross, held = cross_call(n, count, delta_rows, y)
    coeffs, ys = share_call(n, count, chosen, other, solve_call(gram, cross), held)
    return update_call(present, ys, coeffs, serving)


def solution(mesh):
    return jax.shard_map(
        functools.partial(local, mesh.shape["fsdp"], mesh.shape["ep"]),
        mesh=mesh,
        in_specs=(P("ep", "fsdp", None), P(), P(), P("ep", "fsdp", None)),
        out_specs=P("ep", "fsdp", None),
        check_vma=False,
    )
```

```python
import functools

import jax
import jax.numpy as jnp
from jax import lax
from jax.experimental import pallas as pl
from jax.experimental.pallas import tpu as pltpu
from jax.sharding import PartitionSpec as P

D = 7168
POWER = 2
MESH = pl.DeviceIdType.MESH
CHUNK = 128
VMEM_LIMIT = 56 * 1024 * 1024
F32 = jnp.float32
BF16 = jnp.bfloat16


def flip(me, bits):
    for bit in bits:
        me = me + (1 - 2 * lax.rem(lax.div(me, 1 << bit), 2)) * (1 << bit)
    return me


def digits(count):
    return list(range(count.bit_length() - 1))


def greet(me, n, own=None, bits=()):
    barrier = pltpu.get_barrier_semaphore()
    for bit in bits:
        pl.semaphore_signal(barrier, inc=1, device_id={"ep": flip(own, [bit])}, device_id_type=MESH)
    peers = len(bits)
    if n > 0:
        @pl.when(me > 0)
        def _():
            pl.semaphore_signal(barrier, inc=1, device_id={"fsdp": me - 1}, device_id_type=MESH)

        @pl.when(me < n - 1)
        def _():
            pl.semaphore_signal(barrier, inc=1, device_id={"fsdp": me + 1}, device_id_type=MESH)

        peers = peers + (me > 0).astype(jnp.int32) + (me < n - 1).astype(jnp.int32)
    pl.semaphore_wait(barrier, peers)


class Cube:
    def __init__(self, own, order, at, ssem, rsem):
        self.own, self.order, self.at, self.ssem, self.rsem = own, order, at, ssem, rsem

    def copy(self, held, bit, index):
        block = self.at(lax.div(flip(self.own, held), 2))
        return pltpu.make_async_remote_copy(
            src_ref=block, dst_ref=block, send_sem=self.ssem.at[index], recv_sem=self.rsem.at[index],
            device_id={"ep": flip(self.own, [bit])}, device_id_type=MESH)

    def across(self, stage):
        sets = [[]]
        for bit in self.order[:stage]:
            sets = sets + [one + [bit] for one in sets]
        return [(one, self.order[stage], (1 << stage) - 1 + i) for i, one in enumerate(sets)]

    def run(self, stage):
        if stage > 0:
            for one, bit, index in self.across(stage - 1):
                self.copy(one + [bit], bit, index).wait_recv()
        if stage < len(self.order):
            for plan in self.across(stage):
                self.copy(*plan).start()

    def finish(self):
        for stage in range(len(self.order)):
            for plan in self.across(stage):
                self.copy(*plan).wait_send()


def cubes(own, count, ref, ssem, rsem):
    inner = digits(count)[1:]
    half = ref.shape[1] // 2
    return [
        Cube(own, order, lambda e, h=h: ref.at[e, pl.ds(h * half, half)], ssem.at[h], rsem.at[h])
        for h, order in enumerate((inner, inner[::-1]))
    ]


def moves(me, n, part, bufs, ssem, rsem):
    send_r, send_l, recv_l, recv_r = bufs
    def to_right(j):
        return pltpu.make_async_remote_copy(
            src_ref=send_r.at[j], dst_ref=recv_l.at[j], send_sem=ssem.at[0, j],
            recv_sem=rsem.at[0, j], device_id={"fsdp": jnp.minimum(me + 1, n - 1)}, device_id_type=MESH)

    def to_left(j):
        return pltpu.make_async_remote_copy(
            src_ref=send_l.at[j], dst_ref=recv_r.at[j], send_sem=ssem.at[1, j],
            recv_sem=rsem.at[1, j], device_id={"fsdp": jnp.maximum(me - 1, 0)}, device_id_type=MESH)

    @pl.when(me == 0)
    def _():
        recv_l[...] = jnp.zeros_like(recv_l)

    @pl.when(me == n - 1)
    def _():
        recv_r[...] = jnp.zeros_like(recv_r)

    def rightward(j):
        @pl.when(me > 0)
        def _():
            to_right(j).wait_recv()

        @pl.when(me < n - 1)
        def _():
            send_r[j] = (part[j] + recv_l[j].astype(F32)).astype(send_r.dtype)
            to_right(j).start()

    def leftward(j):
        @pl.when(me < n - 1)
        def _():
            to_left(j).wait_recv()

        @pl.when(me > 0)
        def _():
            send_l[j] = (part[j] + recv_r[j].astype(F32)).astype(send_l.dtype)
            to_left(j).start()

    def total(j):
        return part[j] + recv_l[j].astype(F32) + recv_r[j].astype(F32)

    def drain(j, carry):
        @pl.when(me < n - 1)
        def _():
            to_right(j).wait_send()

        @pl.when(me > 0)
        def _():
            to_left(j).wait_send()

        return carry

    return rightward, leftward, total, drain


def chain_sum(me, n, chunks, part, compute, emit, bufs, ssem, rsem, first=None):
    lower = me < n // 2
    edge = jnp.minimum(me, n - 1 - me)
    skew = jnp.where(edge == 0, chunks, jnp.minimum(n - 2 * edge, chunks))
    rightward, leftward, total, drain = moves(me, n, part, bufs, ssem, rsem)
    if first is not None:
        fpart, fcompute, femit, fbufs, fssem, frsem = first
        frightward, fleftward, ftotal, fdrain = moves(me, n, fpart, fbufs, fssem, frsem)

    def step(t, carry):
        if first is not None:
            @pl.when(t == 0)
            def _():
                fpart[0] = fcompute()

                @pl.when(lower)
                def _():
                    frightward(0)

                @pl.when(jnp.logical_not(lower))
                def _():
                    fleftward(0)

            @pl.when(t == skew)
            def _():
                @pl.when(lower)
                def _():
                    fleftward(0)

                @pl.when(jnp.logical_not(lower))
                def _():
                    frightward(0)

                femit(ftotal(0))

        @pl.when(t < chunks)
        def _():
            part[t] = compute(t)

            @pl.when(lower)
            def _():
                rightward(t)

            @pl.when(jnp.logical_not(lower))
            def _():
                leftward(t)

        @pl.when((t >= skew) & (t < skew + chunks))
        def _():
            j = t - skew

            @pl.when(lower)
            def _():
                leftward(j)

            @pl.when(jnp.logical_not(lower))
            def _():
                rightward(j)

            emit(j, total(j))

        return carry

    lax.fori_loop(0, 2 * chunks, step, 0)

    lax.fori_loop(0, chunks, drain, 0)
    if first is not None:
        fdrain(0, 0)


def sketch_kernel(n, count, tile, chunks, a_ref, w_ref, gram_ref, cross_ref, ys_ref, y_ref, yt, p, part, gpart,
                  gsend_r, gsend_l, grecv_l, grecv_r, send_r, send_l, recv_l, recv_r,
                  gssem, grsem, ssem, rsem, cssem, crsem, own_sem):
    me, own = lax.axis_index("fsdp"), lax.axis_index("ep")
    rows = a_ref.shape[0]
    bits = digits(count)
    greet(me, n, own, bits)

    def sketch(weights):
        def body(i, carry):
            at = pl.ds(pl.multiple_of(i * tile, tile), tile)
            block = jnp.dot(a_ref[at, :], weights[...], preferred_element_type=F32)
            y_ref[at, :] = block.astype(BF16)
            yt[:, at] = block.T.astype(BF16)
            return carry

        lax.fori_loop(0, rows // tile, body, 0)

    def compute(j):
        at = pl.ds(pl.multiple_of(j * CHUNK, CHUNK), CHUNK)
        return jnp.dot(yt[...], a_ref[:, at], preferred_element_type=F32)

    def power_emit(j, total):
        at = pl.ds(pl.multiple_of(j * CHUNK, CHUNK), CHUNK)
        p[at, :] = (total / D).T.astype(BF16)

    def bufs(i):
        return [b.at[i] for b in (send_r, send_l, recv_l, recv_r)]

    sketch(w_ref)
    for i in range(POWER):
        chain_sum(me, n, chunks, part, compute, power_emit, bufs(i), ssem.at[i], rsem.at[i])
        sketch(p)

    place = pltpu.make_async_copy(y_ref, ys_ref.at[lax.div(own, 2)], own_sem)
    place.start()
    place.wait()
    gathers = cubes(own, count, ys_ref, cssem, crsem)
    stages = len(bits) - 1
    for gather in gathers:
        gather.run(0)

    def cross_emit(j, total):
        at = pl.ds(pl.multiple_of(j * CHUNK, CHUNK), CHUNK)
        cross_ref[:, at] = total

        @pl.when(j == chunks // 4)
        def _():
            for gather in gathers:
                gather.run(1)

    def gcompute():
        return jnp.dot(yt[...], y_ref[...], preferred_element_type=F32)

    def gemit(total):
        gram_ref[...] = total

    chain_sum(me, n, chunks, part, compute, cross_emit, bufs(POWER), ssem.at[POWER], rsem.at[POWER],
              (gpart, gcompute, gemit, (gsend_r, gsend_l, grecv_l, grecv_r), gssem, grsem))
    for stage in range(2, stages + 1):
        for gather in gathers:
            gather.run(stage)
    for gather in gathers:
        gather.finish()


def sketch_call(n, count, deltas, weights):
    rows, ff = deltas.shape
    rank = weights.shape[1]
    tile = 256 if rows % 256 == 0 else 128
    chunks = ff // CHUNK
    comm = pltpu.VMEM((POWER + 1, chunks, rank, CHUNK), BF16)
    gcomm = pltpu.VMEM((1, rank, rank), F32)
    vmem = pl.BlockSpec(memory_space=pltpu.VMEM)
    dma = pltpu.SemaphoreType.DMA
    return pl.pallas_call(
        functools.partial(sketch_kernel, n, count, tile, chunks),
        out_shape=(
            jax.ShapeDtypeStruct((rank, rank), F32),
            jax.ShapeDtypeStruct((rank, ff), F32),
            jax.ShapeDtypeStruct((count // 2, rows, rank), BF16),
        ),
        in_specs=[vmem, vmem],
        out_specs=(vmem, vmem, pl.BlockSpec(memory_space=pl.ANY)),
        scratch_shapes=[
            pltpu.VMEM((rows, rank), BF16),
            pltpu.VMEM((rank, rows), BF16),
            pltpu.VMEM((ff, rank), BF16),
            pltpu.VMEM((chunks, rank, CHUNK), F32),
            gcomm,
            gcomm, gcomm, gcomm, gcomm,
            comm, comm, comm, comm,
            dma((2, 1)), dma((2, 1)),
            dma((POWER + 1, 2, chunks)), dma((POWER + 1, 2, chunks)),
            dma((2, count // 2 - 1)), dma((2, count // 2 - 1)),
            dma,
        ],
        compiler_params=pltpu.CompilerParams(
            collective_id=0, has_side_effects=True, vmem_limit_bytes=VMEM_LIMIT),
        cost_estimate=pl.CostEstimate(
            flops=2 * rows * ff * rank * 6, bytes_accessed=rows * ff * 2, transcendentals=0),
        name="sketch_sums",
    )(deltas, weights)


def share_kernel(n, count, chosen_ref, other_ref, c_ref, yb_ref, c_out, y_out,
                 whole, piece, whole_send, whole_recv, piece_send, piece_recv, rows_z, y_send, y_recv,
                 wssem, wrsem, pssem, prsem, zssem, zrsem, bssem, brsem):
    me, own = lax.axis_index("fsdp"), lax.axis_index("ep")
    parity = lax.rem(own, 2)
    slots, rank, ff = c_out.shape
    half = ff // 2
    width = half // n
    bits = digits(count)
    stages = len(bits) - 1
    greet(me, n, own, bits)

    def beside(src, dst, index):
        return pltpu.make_async_remote_copy(
            src_ref=src, dst_ref=dst, send_sem=bssem.at[index], recv_sem=brsem.at[index],
            device_id={"ep": flip(own, [0])}, device_id_type=MESH)

    def for_partner(held, send):
        for s in range(slots):
            send[s] = held[lax.div(other_ref[s], 2)]

    def mine(held, recv, s):
        return jnp.where(lax.rem(chosen_ref[s], 2) == parity, held[lax.div(chosen_ref[s], 2)], recv[s])

    whole[lax.div(own, 2)] = c_ref[:, :half]
    piece[lax.div(own, 2)] = c_ref[:, pl.ds(pl.multiple_of(half + me * width, width), width)]
    pieces = cubes(own, count, piece, pssem, prsem)
    wholes = cubes(own, count, whole, wssem, wrsem)
    for gather in pieces + wholes:
        gather.run(0)
    for_partner(yb_ref, y_send)
    y_copies = [beside(y_send.at[s], y_recv.at[s], 2 + s) for s in range(slots)]
    y_copies[0].start()
    for stage in range(1, stages):
        for gather in pieces + wholes:
            gather.run(stage)
    for gather in pieces:
        gather.run(stages)
    for_partner(piece, piece_send)
    piece_copy = beside(piece_send, piece_recv, 1)
    piece_copy.start()
    piece_copy.wait_recv()
    for s in range(slots):
        rows_z[me, s] = mine(piece, piece_recv, s)

    def right(block, hop):
        return pltpu.make_async_remote_copy(
            src_ref=rows_z.at[block], dst_ref=rows_z.at[block], send_sem=zssem.at[0, hop], recv_sem=zrsem.at[0, hop],
            device_id={"fsdp": jnp.minimum(me + 1, n - 1)}, device_id_type=MESH)

    def left(block, hop):
        return pltpu.make_async_remote_copy(
            src_ref=rows_z.at[block], dst_ref=rows_z.at[block], send_sem=zssem.at[1, hop], recv_sem=zrsem.at[1, hop],
            device_id={"fsdp": jnp.maximum(me - 1, 0)}, device_id_type=MESH)

    def send(hop, act):
        @pl.when((me - hop >= 0) & (me < n - 1))
        def _():
            act(right(me - hop, hop))

        @pl.when((me + hop <= n - 1) & (me > 0))
        def _():
            act(left(me + hop, hop))

    def receive(hop):
        @pl.when(me - 1 - hop >= 0)
        def _():
            right(me - 1 - hop, hop).wait_recv()

        @pl.when(me + 1 + hop <= n - 1)
        def _():
            left(me + 1 + hop, hop).wait_recv()

    send(0, lambda copy: copy.start())
    for copy in y_copies[1:]:
        copy.start()
    whole_copy = beside(whole_send, whole_recv, 0)
    for hop in range(n - 1):
        receive(hop)
        if hop < n - 2:
            send(hop + 1, lambda copy: copy.start())
        if hop == 0:
            for gather in wholes:
                gather.run(stages)
            for_partner(whole, whole_send)
            whole_copy.start()
    for s in range(slots):
        y_copies[s].wait_recv()
        y_out[s] = mine(yb_ref, y_recv, s)
    whole_copy.wait_recv()
    for s in range(slots):
        c_out[s, :, :half] = mine(whole, whole_recv, s)
        for z in range(n):
            c_out[s, :, half + z * width:half + (z + 1) * width] = rows_z[z, s]
    for gather in pieces + wholes:
        gather.finish()
    for copy in y_copies + [piece_copy, whole_copy]:
        copy.wait_send()
    for hop in range(n - 1):
        send(hop, lambda copy: copy.wait_send())


def share_call(n, count, chosen, other, coeffs, held):
    rank, ff = coeffs.shape
    rows = held.shape[1]
    slots = chosen.shape[0]
    half, width = ff // 2, ff // 2 // n
    vmem = pl.BlockSpec(memory_space=pltpu.VMEM)
    smem = pl.BlockSpec(memory_space=pltpu.SMEM)
    dma = pltpu.SemaphoreType.DMA
    return pl.pallas_call(
        functools.partial(share_kernel, n, count),
        out_shape=(
            jax.ShapeDtypeStruct((slots, rank, ff), BF16),
            jax.ShapeDtypeStruct((slots, rows, rank), BF16),
        ),
        in_specs=[smem, smem, vmem, vmem],
        out_specs=(vmem, vmem),
        scratch_shapes=[
            pltpu.VMEM((count // 2, rank, half), BF16),
            pltpu.VMEM((count // 2, rank, width), BF16),
            pltpu.VMEM((slots, rank, half), BF16),
            pltpu.VMEM((slots, rank, half), BF16),
            pltpu.VMEM((slots, rank, width), BF16),
            pltpu.VMEM((slots, rank, width), BF16),
            pltpu.VMEM((n, slots, rank, width), BF16),
            pltpu.VMEM((slots, rows, rank), BF16),
            pltpu.VMEM((slots, rows, rank), BF16),
            dma((2, count // 2 - 1)), dma((2, count // 2 - 1)),
            dma((2, count // 2 - 1)), dma((2, count // 2 - 1)),
            dma((2, n - 1)), dma((2, n - 1)),
            dma((2 + slots,)), dma((2 + slots,)),
        ],
        compiler_params=pltpu.CompilerParams(
            collective_id=1, has_side_effects=True, vmem_limit_bytes=VMEM_LIMIT),
        name="share_chosen",
    )(chosen, other, coeffs, held)


def mul(a, b):
    return jnp.dot(a, b, preferred_element_type=F32, precision=lax.Precision.HIGHEST)


def solve_kernel(gram_ref, cross_ref, out_ref, g_ref, x_ref):
    gram = gram_ref[...]
    rank = gram.shape[0]
    eye = lax.broadcasted_iota(jnp.int32, gram.shape, 0) == lax.broadcasted_iota(jnp.int32, gram.shape, 1)
    one = jnp.where(eye, F32(1), F32(0))
    diag = jnp.where(eye, gram, F32(0))
    down = lax.rsqrt(jnp.sum(diag, axis=1, keepdims=True))
    across = lax.rsqrt(jnp.sum(diag, axis=0, keepdims=True))
    g = gram * down * across
    g_ref[...] = g
    start = one / jnp.max(jnp.sum(jnp.abs(g), axis=1))
    x_ref[...] = start

    def rough(carry):
        count, _ = carry
        x = x_ref[...]
        low = x.astype(BF16)
        miss = one - jnp.dot(g_ref[...].astype(BF16), low, preferred_element_type=F32)
        x_ref[...] = x + jnp.dot(low, miss.astype(BF16), preferred_element_type=F32)
        return count + 1, jnp.sum(miss * miss)

    lax.while_loop(lambda c: (c[0] < 16) & (c[1] > 0.3), rough, (jnp.int32(0), F32(1e9)))
    miss = one - mul(g_ref[...], x_ref[...])
    sound = jnp.sum(miss * miss) < 0.9

    @pl.when(jnp.logical_not(sound))
    def _():
        x_ref[...] = start

    def newton(carry):
        count, _ = carry
        x = x_ref[...]
        miss = one - mul(g_ref[...], x)
        x_ref[...] = x + mul(x, miss)
        return count + 1, jnp.sum(miss * miss)

    lax.while_loop(lambda c: (c[0] < 64) & (c[1] > 1e-6), newton, (jnp.int32(0), F32(1e9)))
    out_ref[...] = (mul(x_ref[...], cross_ref[...] * down) * down).astype(BF16)


def solve_call(gram, cross):
    vmem = pl.BlockSpec(memory_space=pltpu.VMEM)
    return pl.pallas_call(
        solve_kernel,
        out_shape=jax.ShapeDtypeStruct(cross.shape, BF16),
        in_specs=[vmem, vmem],
        out_specs=vmem,
        scratch_shapes=[pltpu.VMEM(gram.shape, F32), pltpu.VMEM(gram.shape, F32)],
        compiler_params=pltpu.CompilerParams(vmem_limit_bytes=VMEM_LIMIT),
        cost_estimate=pl.CostEstimate(flops=10 * 10**9, bytes_accessed=10**6, transcendentals=0),
        name="solve",
    )(gram, cross)


def update_kernel(present_ref, y_ref, c_ref, serving_ref, out_ref):
    y = jnp.where(present_ref[pl.program_id(0)] == 1, y_ref[0].astype(F32), F32(0)).astype(BF16)
    tile, ff = y.shape[0], c_ref.shape[2]
    for at in range(0, ff, 256):
        columns = slice(at, at + 256)
        for top in range(0, tile, tile // 2):
            rows = slice(top, top + tile // 2)
            update = jnp.dot(y[rows], c_ref[0, :, columns], preferred_element_type=F32)
            out_ref[0, rows, columns] = (serving_ref[0, rows, columns].astype(F32) + update).astype(BF16)


def update_call(present, ys, coeffs, serving):
    slots, rows, ff = serving.shape
    rank = ys.shape[2]
    tile = rows // 4
    return pl.pallas_call(
        update_kernel,
        out_shape=jax.ShapeDtypeStruct(serving.shape, BF16),
        grid_spec=pltpu.PrefetchScalarGridSpec(
            num_scalar_prefetch=1,
            grid=(slots, rows // tile),
            in_specs=[
                pl.BlockSpec((1, tile, rank), lambda s, i, p: (s, i, 0)),
                pl.BlockSpec((1, rank, ff), lambda s, i, p: (s, 0, 0)),
                pl.BlockSpec((1, tile, ff), lambda s, i, p: (s, i, 0)),
            ],
            out_specs=pl.BlockSpec((1, tile, ff), lambda s, i, p: (s, i, 0)),
        ),
        compiler_params=pltpu.CompilerParams(vmem_limit_bytes=VMEM_LIMIT),
        cost_estimate=pl.CostEstimate(
            flops=2 * slots * rows * ff * rank, bytes_accessed=4 * slots * rows * ff, transcendentals=0),
        name="update",
    )(present, ys, coeffs, serving)


def local(n, count, deltas, sketch_matrix, owner_of, serving):
    slot_count = serving.shape[0]
    own_index = lax.axis_index("ep")
    delta_rows = deltas[0]

    def slots_of(owner):
        is_owned = (owner_of == owner).astype(jnp.int32)
        owned_rank = jnp.cumsum(is_owned, dtype=jnp.int32) - 1
        slot_ids = jnp.arange(slot_count, dtype=jnp.int32)
        hits = (is_owned[None, :] == 1) & (owned_rank[None, :] == slot_ids[:, None])
        expert_ids = jnp.arange(owner_of.shape[0], dtype=jnp.int32)
        chosen = jnp.sum(jnp.where(hits, expert_ids[None, :], 0), axis=1).astype(jnp.int32)
        return chosen, jnp.any(hits, axis=1).astype(jnp.int32)

    chosen, present = slots_of(own_index)
    other, _ = slots_of(flip(own_index, [0]))

    gram, cross, held = sketch_call(n, count, delta_rows, sketch_matrix)
    coeffs, ys = share_call(n, count, chosen, other, solve_call(gram, cross), held)
    return update_call(present, ys, coeffs, serving)


def solution(mesh):
    return jax.shard_map(
        functools.partial(local, mesh.shape["fsdp"], mesh.shape["ep"]),
        mesh=mesh,
        in_specs=(P("ep", "fsdp", None), P(), P(), P("ep", "fsdp", None)),
        out_specs=P("ep", "fsdp", None),
        check_vma=False,
    )
```

```python
import functools

import jax
import jax.numpy as jnp
from jax import lax
from jax.experimental import pallas as pl
from jax.experimental.pallas import tpu as pltpu
from jax.sharding import PartitionSpec as P

D = 7168
POWER = 2
MESH = pl.DeviceIdType.MESH
CHUNK = 128
PIECES = 4
VMEM_LIMIT = 56 * 1024 * 1024
F32 = jnp.float32
BF16 = jnp.bfloat16


def flip(me, bits):
    for bit in bits:
        me = me + (1 - 2 * lax.rem(lax.div(me, 1 << bit), 2)) * (1 << bit)
    return me


def digits(count):
    return list(range(count.bit_length() - 1))


def greet(me, n, own=None, bits=()):
    barrier = pltpu.get_barrier_semaphore()
    for bit in bits:
        pl.semaphore_signal(barrier, inc=1, device_id={"ep": flip(own, [bit])}, device_id_type=MESH)
    peers = len(bits)
    if n > 0:
        @pl.when(me > 0)
        def _():
            pl.semaphore_signal(barrier, inc=1, device_id={"fsdp": me - 1}, device_id_type=MESH)

        @pl.when(me < n - 1)
        def _():
            pl.semaphore_signal(barrier, inc=1, device_id={"fsdp": me + 1}, device_id_type=MESH)

        peers = peers + (me > 0).astype(jnp.int32) + (me < n - 1).astype(jnp.int32)
    pl.semaphore_wait(barrier, peers)


class Cube:
    def __init__(self, own, order, at, ssem, rsem):
        self.own, self.order, self.at, self.ssem, self.rsem = own, order, at, ssem, rsem

    def copy(self, held, bit, index):
        block = self.at(lax.div(flip(self.own, held), 2))
        return pltpu.make_async_remote_copy(
            src_ref=block, dst_ref=block, send_sem=self.ssem.at[index], recv_sem=self.rsem.at[index],
            device_id={"ep": flip(self.own, [bit])}, device_id_type=MESH)

    def across(self, stage):
        sets = [[]]
        for bit in self.order[:stage]:
            sets = sets + [one + [bit] for one in sets]
        return [(one, self.order[stage], (1 << stage) - 1 + i) for i, one in enumerate(sets)]

    def run(self, stage):
        if stage > 0:
            for one, bit, index in self.across(stage - 1):
                self.copy(one + [bit], bit, index).wait_recv()
        if stage < len(self.order):
            for plan in self.across(stage):
                self.copy(*plan).start()

    def finish(self):
        for stage in range(len(self.order)):
            for plan in self.across(stage):
                self.copy(*plan).wait_send()


def cubes(own, count, ref, ssem, rsem):
    inner = digits(count)[1:]
    half = ref.shape[1] // 2
    return [
        Cube(own, order, lambda e, h=h: ref.at[e, pl.ds(h * half, half)], ssem.at[h], rsem.at[h])
        for h, order in enumerate((inner, inner[::-1]))
    ]


def moves(me, n, part, bufs, ssem, rsem):
    send_r, send_l, recv_l, recv_r = bufs
    def to_right(j):
        return pltpu.make_async_remote_copy(
            src_ref=send_r.at[j], dst_ref=recv_l.at[j], send_sem=ssem.at[0, j],
            recv_sem=rsem.at[0, j], device_id={"fsdp": jnp.minimum(me + 1, n - 1)}, device_id_type=MESH)

    def to_left(j):
        return pltpu.make_async_remote_copy(
            src_ref=send_l.at[j], dst_ref=recv_r.at[j], send_sem=ssem.at[1, j],
            recv_sem=rsem.at[1, j], device_id={"fsdp": jnp.maximum(me - 1, 0)}, device_id_type=MESH)

    @pl.when(me == 0)
    def _():
        recv_l[...] = jnp.zeros_like(recv_l)

    @pl.when(me == n - 1)
    def _():
        recv_r[...] = jnp.zeros_like(recv_r)

    def rightward(j):
        @pl.when(me > 0)
        def _():
            to_right(j).wait_recv()

        @pl.when(me < n - 1)
        def _():
            send_r[j] = (part[j] + recv_l[j].astype(F32)).astype(send_r.dtype)
            to_right(j).start()

    def leftward(j):
        @pl.when(me < n - 1)
        def _():
            to_left(j).wait_recv()

        @pl.when(me > 0)
        def _():
            send_l[j] = (part[j] + recv_r[j].astype(F32)).astype(send_l.dtype)
            to_left(j).start()

    def total(j):
        return part[j] + recv_l[j].astype(F32) + recv_r[j].astype(F32)

    def drain(j, carry):
        @pl.when(me < n - 1)
        def _():
            to_right(j).wait_send()

        @pl.when(me > 0)
        def _():
            to_left(j).wait_send()

        return carry

    return rightward, leftward, total, drain


def chain_sum(me, n, chunks, part, compute, emit, bufs, ssem, rsem, first=None):
    lower = me < n // 2
    edge = jnp.minimum(me, n - 1 - me)
    skew = jnp.where(edge == 0, chunks, jnp.minimum(n - 2 * edge, chunks))
    rightward, leftward, total, drain = moves(me, n, part, bufs, ssem, rsem)
    if first is not None:
        fpart, fcompute, femit, fbufs, fssem, frsem = first
        pieces = fpart.shape[0]
        frightward, fleftward, ftotal, fdrain = moves(me, n, fpart, fbufs, fssem, frsem)

    def step(t, carry):
        if first is not None:
            @pl.when(t < pieces)
            def _():
                fpart[t] = fcompute(t)

                @pl.when(lower)
                def _():
                    frightward(t)

                @pl.when(jnp.logical_not(lower))
                def _():
                    fleftward(t)

            @pl.when((t >= skew) & (t < skew + pieces))
            def _():
                i = t - skew

                @pl.when(lower)
                def _():
                    fleftward(i)

                @pl.when(jnp.logical_not(lower))
                def _():
                    frightward(i)

                femit(i, ftotal(i))

        @pl.when(t < chunks)
        def _():
            part[t] = compute(t)

            @pl.when(lower)
            def _():
                rightward(t)

            @pl.when(jnp.logical_not(lower))
            def _():
                leftward(t)

        @pl.when((t >= skew) & (t < skew + chunks))
        def _():
            j = t - skew

            @pl.when(lower)
            def _():
                leftward(j)

            @pl.when(jnp.logical_not(lower))
            def _():
                rightward(j)

            emit(j, total(j))

        return carry

    lax.fori_loop(0, 2 * chunks, step, 0)

    lax.fori_loop(0, chunks, drain, 0)
    if first is not None:
        lax.fori_loop(0, pieces, fdrain, 0)


def sketch_kernel(n, count, tile, chunks, a_hbm, w_ref, gram_ref, cross_ref, ys_ref, a_ref, a_sem, y_ref, yt, p, part, gpart,
                  gsend_r, gsend_l, grecv_l, grecv_r, send_r, send_l, recv_l, recv_r,
                  gssem, grsem, ssem, rsem, cssem, crsem, own_sem):
    me, own = lax.axis_index("fsdp"), lax.axis_index("ep")
    rows = a_ref.shape[0]
    bits = digits(count)

    def load(i):
        at = pl.ds(pl.multiple_of(i * tile, tile), tile)
        return pltpu.make_async_copy(a_hbm.at[at], a_ref.at[at], a_sem.at[i])

    def begin(i, carry):
        load(i).start()
        return carry

    lax.fori_loop(0, rows // tile, begin, 0)
    greet(me, n, own, bits)

    def sketch(weights, loading=False):
        def body(i, carry):
            at = pl.ds(pl.multiple_of(i * tile, tile), tile)
            if loading:
                load(i).wait()
            block = jnp.dot(a_ref[at, :], weights[...], preferred_element_type=F32)
            y_ref[at, :] = block.astype(BF16)
            yt[:, at] = block.T.astype(BF16)
            return carry

        lax.fori_loop(0, rows // tile, body, 0)

    def compute(j):
        at = pl.ds(pl.multiple_of(j * CHUNK, CHUNK), CHUNK)
        return jnp.dot(yt[...], a_ref[:, at], preferred_element_type=F32)

    def power_emit(j, total):
        at = pl.ds(pl.multiple_of(j * CHUNK, CHUNK), CHUNK)
        p[at, :] = (total / D).T.astype(BF16)

    def bufs(i):
        return [b.at[i] for b in (send_r, send_l, recv_l, recv_r)]

    sketch(w_ref, True)
    for i in range(POWER):
        chain_sum(me, n, chunks, part, compute, power_emit, bufs(i), ssem.at[i], rsem.at[i])
        sketch(p)

    place = pltpu.make_async_copy(y_ref, ys_ref.at[lax.div(own, 2)], own_sem)
    place.start()
    place.wait()
    gathers = cubes(own, count, ys_ref, cssem, crsem)
    stages = len(bits) - 1
    for gather in gathers:
        gather.run(0)

    def cross_emit(j, total):
        at = pl.ds(pl.multiple_of(j * CHUNK, CHUNK), CHUNK)
        cross_ref[:, at] = total

        edge = (me == 0) | (me == n - 1)

        @pl.when(j == jnp.where(edge, 0, chunks // 4))
        def _():
            for gather in gathers:
                gather.run(1)

    band = gpart.shape[1]

    def gcompute(i):
        at = pl.ds(pl.multiple_of(i * band, band), band)
        return jnp.dot(yt[at, :], y_ref[...], preferred_element_type=F32)

    def gemit(i, total):
        gram_ref[pl.ds(pl.multiple_of(i * band, band), band), :] = total

    chain_sum(me, n, chunks, part, compute, cross_emit, bufs(POWER), ssem.at[POWER], rsem.at[POWER],
              (gpart, gcompute, gemit, (gsend_r, gsend_l, grecv_l, grecv_r), gssem, grsem))
    for stage in range(2, stages + 1):
        for gather in gathers:
            gather.run(stage)
    for gather in gathers:
        gather.finish()


def sketch_call(n, count, deltas, weights):
    rows, ff = deltas.shape
    rank = weights.shape[1]
    tile = 256 if rows % 256 == 0 else 128
    chunks = ff // CHUNK
    comm = pltpu.VMEM((POWER + 1, chunks, rank, CHUNK), BF16)
    gcomm = pltpu.VMEM((PIECES, rank // PIECES, rank), F32)
    vmem = pl.BlockSpec(memory_space=pltpu.VMEM)
    dma = pltpu.SemaphoreType.DMA
    return pl.pallas_call(
        functools.partial(sketch_kernel, n, count, tile, chunks),
        out_shape=(
            jax.ShapeDtypeStruct((rank, rank), F32),
            jax.ShapeDtypeStruct((rank, ff), F32),
            jax.ShapeDtypeStruct((count // 2, rows, rank), BF16),
        ),
        in_specs=[pl.BlockSpec(memory_space=pl.ANY), vmem],
        out_specs=(vmem, vmem, pl.BlockSpec(memory_space=pl.ANY)),
        scratch_shapes=[
            pltpu.VMEM((rows, ff), BF16),
            dma((rows // tile,)),
            pltpu.VMEM((rows, rank), BF16),
            pltpu.VMEM((rank, rows), BF16),
            pltpu.VMEM((ff, rank), BF16),
            pltpu.VMEM((chunks, rank, CHUNK), F32),
            gcomm,
            gcomm, gcomm, gcomm, gcomm,
            comm, comm, comm, comm,
            dma((2, PIECES)), dma((2, PIECES)),
            dma((POWER + 1, 2, chunks)), dma((POWER + 1, 2, chunks)),
            dma((2, count // 2 - 1)), dma((2, count // 2 - 1)),
            dma,
        ],
        compiler_params=pltpu.CompilerParams(
            collective_id=0, has_side_effects=True, vmem_limit_bytes=VMEM_LIMIT),
        cost_estimate=pl.CostEstimate(
            flops=2 * rows * ff * rank * 6, bytes_accessed=rows * ff * 2, transcendentals=0),
        name="sketch_sums",
    )(deltas, weights)


def share_kernel(n, count, owner_ref, c_ref, yb_ref, c_out, y_out,
                 whole, piece, whole_send, whole_recv, piece_send, piece_recv, rows_z, y_send, y_recv,
                 wssem, wrsem, pssem, prsem, zssem, zrsem, bssem, brsem):
    me, own = lax.axis_index("fsdp"), lax.axis_index("ep")
    parity = lax.rem(own, 2)
    slots, rank, ff = c_out.shape
    half = ff // 2
    width = half // n
    bits = digits(count)
    stages = len(bits) - 1
    greet(me, n, own, bits)

    def slots_of(owner):
        seen, chosen, present = jnp.int32(0), [jnp.int32(0)] * slots, [jnp.int32(0)] * slots
        for expert in range(count):
            owned = (owner_ref[expert] == owner).astype(jnp.int32)
            for s in range(slots):
                hit = owned * (seen == s).astype(jnp.int32)
                chosen[s] = chosen[s] + hit * expert
                present[s] = present[s] + hit
            seen = seen + owned
        return chosen, present

    chosen, present = slots_of(own)
    other, _ = slots_of(flip(own, [0]))

    def beside(src, dst, index):
        return pltpu.make_async_remote_copy(
            src_ref=src, dst_ref=dst, send_sem=bssem.at[index], recv_sem=brsem.at[index],
            device_id={"ep": flip(own, [0])}, device_id_type=MESH)

    def for_partner(held, send):
        for s in range(slots):
            send[s] = held[lax.div(other[s], 2)]

    def mine(held, recv, s):
        return jnp.where(lax.rem(chosen[s], 2) == parity, held[lax.div(chosen[s], 2)], recv[s])

    whole[lax.div(own, 2)] = c_ref[:, :half]
    piece[lax.div(own, 2)] = c_ref[:, pl.ds(pl.multiple_of(half + me * width, width), width)]
    pieces = cubes(own, count, piece, pssem, prsem)
    wholes = cubes(own, count, whole, wssem, wrsem)
    for gather in pieces:
        gather.run(0)
    for gather in pieces:
        gather.run(1)
    for gather in wholes:
        gather.run(0)
    for_partner(yb_ref, y_send)
    y_copies = [beside(y_send.at[s], y_recv.at[s], 2 + s) for s in range(slots)]
    y_copies[0].start()
    for stage in range(2, stages + 1):
        for gather in pieces:
            gather.run(stage)
    for_partner(piece, piece_send)
    piece_copy = beside(piece_send, piece_recv, 1)
    piece_copy.start()
    for stage in range(1, stages):
        for gather in wholes:
            gather.run(stage)
    piece_copy.wait_recv()
    for s in range(slots):
        rows_z[me, s] = mine(piece, piece_recv, s)

    def right(block, hop):
        return pltpu.make_async_remote_copy(
            src_ref=rows_z.at[block], dst_ref=rows_z.at[block], send_sem=zssem.at[0, hop], recv_sem=zrsem.at[0, hop],
            device_id={"fsdp": jnp.minimum(me + 1, n - 1)}, device_id_type=MESH)

    def left(block, hop):
        return pltpu.make_async_remote_copy(
            src_ref=rows_z.at[block], dst_ref=rows_z.at[block], send_sem=zssem.at[1, hop], recv_sem=zrsem.at[1, hop],
            device_id={"fsdp": jnp.maximum(me - 1, 0)}, device_id_type=MESH)

    def send(hop, act):
        @pl.when((me - hop >= 0) & (me < n - 1))
        def _():
            act(right(me - hop, hop))

        @pl.when((me + hop <= n - 1) & (me > 0))
        def _():
            act(left(me + hop, hop))

    def receive(hop):
        @pl.when(me - 1 - hop >= 0)
        def _():
            right(me - 1 - hop, hop).wait_recv()

        @pl.when(me + 1 + hop <= n - 1)
        def _():
            left(me + 1 + hop, hop).wait_recv()

    send(0, lambda copy: copy.start())
    for copy in y_copies[1:]:
        copy.start()
    whole_copy = beside(whole_send, whole_recv, 0)
    for hop in range(n - 1):
        receive(hop)
        if hop < n - 2:
            send(hop + 1, lambda copy: copy.start())
        if hop == 0:
            for gather in wholes:
                gather.run(stages)
            for_partner(whole, whole_send)
            whole_copy.start()
    for s in range(slots):
        y_copies[s].wait_recv()
        y_out[s] = jnp.where(present[s] == 1, mine(yb_ref, y_recv, s), jnp.zeros_like(y_recv[s]))
    whole_copy.wait_recv()
    for s in range(slots):
        c_out[s, :, :half] = mine(whole, whole_recv, s)
        for z in range(n):
            c_out[s, :, half + z * width:half + (z + 1) * width] = rows_z[z, s]
    for gather in pieces + wholes:
        gather.finish()
    for copy in y_copies + [piece_copy, whole_copy]:
        copy.wait_send()
    for hop in range(n - 1):
        send(hop, lambda copy: copy.wait_send())


def share_call(n, count, slots, owner_of, coeffs, held):
    rank, ff = coeffs.shape
    rows = held.shape[1]
    half, width = ff // 2, ff // 2 // n
    vmem = pl.BlockSpec(memory_space=pltpu.VMEM)
    smem = pl.BlockSpec(memory_space=pltpu.SMEM)
    dma = pltpu.SemaphoreType.DMA
    return pl.pallas_call(
        functools.partial(share_kernel, n, count),
        out_shape=(
            jax.ShapeDtypeStruct((slots, rank, ff), BF16),
            jax.ShapeDtypeStruct((slots, rows, rank), BF16),
        ),
        in_specs=[smem, vmem, vmem],
        out_specs=(vmem, vmem),
        scratch_shapes=[
            pltpu.VMEM((count // 2, rank, half), BF16),
            pltpu.VMEM((count // 2, rank, width), BF16),
            pltpu.VMEM((slots, rank, half), BF16),
            pltpu.VMEM((slots, rank, half), BF16),
            pltpu.VMEM((slots, rank, width), BF16),
            pltpu.VMEM((slots, rank, width), BF16),
            pltpu.VMEM((n, slots, rank, width), BF16),
            pltpu.VMEM((slots, rows, rank), BF16),
            pltpu.VMEM((slots, rows, rank), BF16),
            dma((2, count // 2 - 1)), dma((2, count // 2 - 1)),
            dma((2, count // 2 - 1)), dma((2, count // 2 - 1)),
            dma((2, n - 1)), dma((2, n - 1)),
            dma((2 + slots,)), dma((2 + slots,)),
        ],
        compiler_params=pltpu.CompilerParams(
            collective_id=1, has_side_effects=True, vmem_limit_bytes=VMEM_LIMIT),
        name="share_chosen",
    )(owner_of, coeffs, held)


def mul(a, b):
    return jnp.dot(a, b, preferred_element_type=F32, precision=lax.Precision.HIGHEST)


def solve_kernel(gram_ref, cross_ref, out_ref, g_ref, x_ref):
    gram = gram_ref[...]
    rank = gram.shape[0]
    eye = lax.broadcasted_iota(jnp.int32, gram.shape, 0) == lax.broadcasted_iota(jnp.int32, gram.shape, 1)
    one = jnp.where(eye, F32(1), F32(0))
    diag = jnp.where(eye, gram, F32(0))
    down = lax.rsqrt(jnp.sum(diag, axis=1, keepdims=True))
    across = lax.rsqrt(jnp.sum(diag, axis=0, keepdims=True))
    g = gram * down * across
    g_ref[...] = g
    start = one / jnp.max(jnp.sum(jnp.abs(g), axis=1))
    x_ref[...] = start

    def rough(carry):
        count, _ = carry
        x = x_ref[...]
        low = x.astype(BF16)
        miss = one - jnp.dot(g_ref[...].astype(BF16), low, preferred_element_type=F32)
        x_ref[...] = x + jnp.dot(low, miss.astype(BF16), preferred_element_type=F32)
        return count + 1, jnp.sum(miss * miss)

    lax.while_loop(lambda c: (c[0] < 16) & (c[1] > 0.3), rough, (jnp.int32(0), F32(1e9)))
    miss = one - mul(g_ref[...], x_ref[...])
    sound = jnp.sum(miss * miss) < 0.9

    @pl.when(jnp.logical_not(sound))
    def _():
        x_ref[...] = start

    def newton(carry):
        count, _ = carry
        x = x_ref[...]
        miss = one - mul(g_ref[...], x)
        x_ref[...] = x + mul(x, miss)
        return count + 1, jnp.sum(miss * miss)

    lax.while_loop(lambda c: (c[0] < 64) & (c[1] > 1e-6), newton, (jnp.int32(0), F32(1e9)))
    out_ref[...] = (mul(x_ref[...], cross_ref[...] * down) * down).astype(BF16)


def solve_call(gram, cross):
    vmem = pl.BlockSpec(memory_space=pltpu.VMEM)
    return pl.pallas_call(
        solve_kernel,
        out_shape=jax.ShapeDtypeStruct(cross.shape, BF16),
        in_specs=[vmem, vmem],
        out_specs=vmem,
        scratch_shapes=[pltpu.VMEM(gram.shape, F32), pltpu.VMEM(gram.shape, F32)],
        compiler_params=pltpu.CompilerParams(vmem_limit_bytes=VMEM_LIMIT),
        cost_estimate=pl.CostEstimate(flops=10 * 10**9, bytes_accessed=10**6, transcendentals=0),
        name="solve",
    )(gram, cross)


def update_kernel(y_ref, c_ref, serving_ref, out_ref):
    tile, ff = y_ref.shape[1], c_ref.shape[2]
    for at in range(0, ff, 256):
        columns = slice(at, at + 256)
        for top in range(0, tile, tile // 2):
            rows = slice(top, top + tile // 2)
            update = jnp.dot(y_ref[0, rows, :], c_ref[0, :, columns], preferred_element_type=F32)
            out_ref[0, rows, columns] = (serving_ref[0, rows, columns].astype(F32) + update).astype(BF16)


def update_call(ys, coeffs, serving):
    slots, rows, ff = serving.shape
    rank = ys.shape[2]
    tile = rows // 2
    return pl.pallas_call(
        update_kernel,
        out_shape=jax.ShapeDtypeStruct(serving.shape, BF16),
        grid=(slots, rows // tile),
        in_specs=[
            pl.BlockSpec((1, tile, rank), lambda s, i: (s, i, 0)),
            pl.BlockSpec((1, rank, ff), lambda s, i: (s, 0, 0)),
            pl.BlockSpec((1, tile, ff), lambda s, i: (s, i, 0)),
        ],
        out_specs=pl.BlockSpec((1, tile, ff), lambda s, i: (s, i, 0)),
        compiler_params=pltpu.CompilerParams(vmem_limit_bytes=VMEM_LIMIT),
        cost_estimate=pl.CostEstimate(
            flops=2 * slots * rows * ff * rank, bytes_accessed=4 * slots * rows * ff, transcendentals=0),
        name="update",
    )(ys, coeffs, serving)


def local(n, count, deltas, sketch_matrix, owner_of, serving):
    gram, cross, held = sketch_call(n, count, deltas[0], sketch_matrix)
    coeffs, ys = share_call(n, count, serving.shape[0], owner_of, solve_call(gram, cross), held)
    return update_call(ys, coeffs, serving)


def solution(mesh):
    return jax.shard_map(
        functools.partial(local, mesh.shape["fsdp"], mesh.shape["ep"]),
        mesh=mesh,
        in_specs=(P("ep", "fsdp", None), P(), P(), P("ep", "fsdp", None)),
        out_specs=P("ep", "fsdp", None),
        check_vma=False,
    )
```

```python
import functools

import jax
import jax.numpy as jnp
from jax import lax
from jax.experimental import pallas as pl
from jax.experimental.pallas import tpu as pltpu
from jax.sharding import PartitionSpec as P

D = 7168
POWER = 2
MESH = pl.DeviceIdType.MESH
CHUNK = 128
PIECES = 4
VMEM_LIMIT = 56 * 1024 * 1024
F32 = jnp.float32
BF16 = jnp.bfloat16


def flip(me, bits):
    for bit in bits:
        me = me + (1 - 2 * lax.rem(lax.div(me, 1 << bit), 2)) * (1 << bit)
    return me


def digits(count):
    return list(range(count.bit_length() - 1))


def greet(me, n, own=None, bits=()):
    barrier = pltpu.get_barrier_semaphore()
    for bit in bits:
        pl.semaphore_signal(barrier, inc=1, device_id={"ep": flip(own, [bit])}, device_id_type=MESH)
    peers = len(bits)
    if n > 0:
        @pl.when(me > 0)
        def _():
            pl.semaphore_signal(barrier, inc=1, device_id={"fsdp": me - 1}, device_id_type=MESH)

        @pl.when(me < n - 1)
        def _():
            pl.semaphore_signal(barrier, inc=1, device_id={"fsdp": me + 1}, device_id_type=MESH)

        peers = peers + (me > 0).astype(jnp.int32) + (me < n - 1).astype(jnp.int32)
    pl.semaphore_wait(barrier, peers)


class Cube:
    def __init__(self, own, order, at, ssem, rsem):
        self.own, self.order, self.at, self.ssem, self.rsem = own, order, at, ssem, rsem

    def copy(self, held, bit, index):
        block = self.at(lax.div(flip(self.own, held), 2))
        return pltpu.make_async_remote_copy(
            src_ref=block, dst_ref=block, send_sem=self.ssem.at[index], recv_sem=self.rsem.at[index],
            device_id={"ep": flip(self.own, [bit])}, device_id_type=MESH)

    def across(self, stage):
        sets = [[]]
        for bit in self.order[:stage]:
            sets = sets + [one + [bit] for one in sets]
        return [(one, self.order[stage], (1 << stage) - 1 + i) for i, one in enumerate(sets)]

    def run(self, stage):
        if stage > 0:
            for one, bit, index in self.across(stage - 1):
                self.copy(one + [bit], bit, index).wait_recv()
        if stage < len(self.order):
            for plan in self.across(stage):
                self.copy(*plan).start()

    def finish(self):
        for stage in range(len(self.order)):
            for plan in self.across(stage):
                self.copy(*plan).wait_send()


def cubes(own, count, ref, ssem, rsem):
    inner = digits(count)[1:]
    half = ref.shape[1] // 2
    return [
        Cube(own, order, lambda e, h=h: ref.at[e, pl.ds(h * half, half)], ssem.at[h], rsem.at[h])
        for h, order in enumerate((inner, inner[::-1]))
    ]


def moves(me, n, part, bufs, ssem, rsem):
    send_r, send_l, recv_l, recv_r = bufs
    def to_right(j):
        return pltpu.make_async_remote_copy(
            src_ref=send_r.at[j], dst_ref=recv_l.at[j], send_sem=ssem.at[0, j],
            recv_sem=rsem.at[0, j], device_id={"fsdp": jnp.minimum(me + 1, n - 1)}, device_id_type=MESH)

    def to_left(j):
        return pltpu.make_async_remote_copy(
            src_ref=send_l.at[j], dst_ref=recv_r.at[j], send_sem=ssem.at[1, j],
            recv_sem=rsem.at[1, j], device_id={"fsdp": jnp.maximum(me - 1, 0)}, device_id_type=MESH)

    @pl.when(me == 0)
    def _():
        recv_l[...] = jnp.zeros_like(recv_l)

    @pl.when(me == n - 1)
    def _():
        recv_r[...] = jnp.zeros_like(recv_r)

    def rightward(j):
        @pl.when(me > 0)
        def _():
            to_right(j).wait_recv()

        @pl.when(me < n - 1)
        def _():
            send_r[j] = (part[j] + recv_l[j].astype(F32)).astype(send_r.dtype)
            to_right(j).start()

    def leftward(j):
        @pl.when(me < n - 1)
        def _():
            to_left(j).wait_recv()

        @pl.when(me > 0)
        def _():
            send_l[j] = (part[j] + recv_r[j].astype(F32)).astype(send_l.dtype)
            to_left(j).start()

    def total(j):
        return part[j] + recv_l[j].astype(F32) + recv_r[j].astype(F32)

    def drain(j, carry):
        @pl.when(me < n - 1)
        def _():
            to_right(j).wait_send()

        @pl.when(me > 0)
        def _():
            to_left(j).wait_send()

        return carry

    return rightward, leftward, total, drain


def chain_sum(me, n, chunks, part, compute, emit, bufs, ssem, rsem, first=None):
    lower = me < n // 2
    edge = jnp.minimum(me, n - 1 - me)
    skew = jnp.where(edge == 0, chunks, jnp.minimum(n + 2 - 2 * edge, chunks))
    rightward, leftward, total, drain = moves(me, n, part, bufs, ssem, rsem)
    if first is not None:
        fpart, fcompute, femit, fbufs, fssem, frsem = first
        pieces = fpart.shape[0]
        frightward, fleftward, ftotal, fdrain = moves(me, n, fpart, fbufs, fssem, frsem)

    def step(t, carry):
        if first is not None:
            @pl.when(t < pieces)
            def _():
                fpart[t] = fcompute(t)

                @pl.when(lower)
                def _():
                    frightward(t)

                @pl.when(jnp.logical_not(lower))
                def _():
                    fleftward(t)

            @pl.when((t >= skew) & (t < skew + pieces))
            def _():
                i = t - skew

                @pl.when(lower)
                def _():
                    fleftward(i)

                @pl.when(jnp.logical_not(lower))
                def _():
                    frightward(i)

                femit(i, ftotal(i))

        @pl.when(t < chunks)
        def _():
            part[t] = compute(t)

            @pl.when(lower)
            def _():
                rightward(t)

            @pl.when(jnp.logical_not(lower))
            def _():
                leftward(t)

        @pl.when((t >= skew) & (t < skew + chunks))
        def _():
            j = t - skew

            @pl.when(lower)
            def _():
                leftward(j)

            @pl.when(jnp.logical_not(lower))
            def _():
                rightward(j)

            emit(j, total(j))

        return carry

    lax.fori_loop(0, 2 * chunks, step, 0)

    lax.fori_loop(0, chunks, drain, 0)
    if first is not None:
        lax.fori_loop(0, pieces, fdrain, 0)


def sketch_kernel(n, count, tile, chunks, a_hbm, w_ref, gram_ref, cross_ref, ys_ref, a_ref, a_sem, y_ref, yt, p, part, gpart,
                  gsend_r, gsend_l, grecv_l, grecv_r, send_r, send_l, recv_l, recv_r,
                  gssem, grsem, ssem, rsem, cssem, crsem, own_sem):
    me, own = lax.axis_index("fsdp"), lax.axis_index("ep")
    rows = a_ref.shape[0]
    bits = digits(count)

    def load(i):
        at = pl.ds(pl.multiple_of(i * tile, tile), tile)
        return pltpu.make_async_copy(a_hbm.at[at], a_ref.at[at], a_sem.at[i])

    def begin(i, carry):
        load(i).start()
        return carry

    lax.fori_loop(0, rows // tile, begin, 0)
    greet(me, n, own, bits)

    def sketch(weights, loading=False):
        def body(i, carry):
            at = pl.ds(pl.multiple_of(i * tile, tile), tile)
            if loading:
                load(i).wait()
            block = jnp.dot(a_ref[at, :], weights[...], preferred_element_type=F32)
            y_ref[at, :] = block.astype(BF16)
            yt[:, at] = block.T.astype(BF16)
            return carry

        lax.fori_loop(0, rows // tile, body, 0)

    def compute(j):
        at = pl.ds(pl.multiple_of(j * CHUNK, CHUNK), CHUNK)
        return jnp.dot(yt[...], a_ref[:, at], preferred_element_type=F32)

    def power_emit(j, total):
        at = pl.ds(pl.multiple_of(j * CHUNK, CHUNK), CHUNK)
        p[at, :] = (total / D).T.astype(BF16)

    def bufs(i):
        return [b.at[i] for b in (send_r, send_l, recv_l, recv_r)]

    sketch(w_ref, True)
    for i in range(POWER):
        chain_sum(me, n, chunks, part, compute, power_emit, bufs(i), ssem.at[i], rsem.at[i])
        sketch(p)

    place = pltpu.make_async_copy(y_ref, ys_ref.at[lax.div(own, 2)], own_sem)
    place.start()
    place.wait()
    gathers = cubes(own, count, ys_ref, cssem, crsem)
    stages = len(bits) - 1
    for gather in gathers:
        gather.run(0)

    def cross_emit(j, total):
        at = pl.ds(pl.multiple_of(j * CHUNK, CHUNK), CHUNK)
        cross_ref[:, at] = total

        edge = (me == 0) | (me == n - 1)

        @pl.when(j == jnp.where(edge, 0, chunks // 4))
        def _():
            for gather in gathers:
                gather.run(1)

    band = gpart.shape[1]

    def gcompute(i):
        at = pl.ds(pl.multiple_of(i * band, band), band)
        return jnp.dot(yt[at, :], y_ref[...], preferred_element_type=F32)

    def gemit(i, total):
        gram_ref[pl.ds(pl.multiple_of(i * band, band), band), :] = total

    chain_sum(me, n, chunks, part, compute, cross_emit, bufs(POWER), ssem.at[POWER], rsem.at[POWER],
              (gpart, gcompute, gemit, (gsend_r, gsend_l, grecv_l, grecv_r), gssem, grsem))
    for stage in range(2, stages + 1):
        for gather in gathers:
            gather.run(stage)
    for gather in gathers:
        gather.finish()


def sketch_call(n, count, deltas, weights):
    rows, ff = deltas.shape
    rank = weights.shape[1]
    tile = 256 if rows % 256 == 0 else 128
    chunks = ff // CHUNK
    comm = pltpu.VMEM((POWER + 1, chunks, rank, CHUNK), BF16)
    gcomm = pltpu.VMEM((PIECES, rank // PIECES, rank), F32)
    vmem = pl.BlockSpec(memory_space=pltpu.VMEM)
    dma = pltpu.SemaphoreType.DMA
    return pl.pallas_call(
        functools.partial(sketch_kernel, n, count, tile, chunks),
        out_shape=(
            jax.ShapeDtypeStruct((rank, rank), F32),
            jax.ShapeDtypeStruct((rank, ff), F32),
            jax.ShapeDtypeStruct((count // 2, rows, rank), BF16),
        ),
        in_specs=[pl.BlockSpec(memory_space=pl.ANY), vmem],
        out_specs=(vmem, vmem, pl.BlockSpec(memory_space=pl.ANY)),
        scratch_shapes=[
            pltpu.VMEM((rows, ff), BF16),
            dma((rows // tile,)),
            pltpu.VMEM((rows, rank), BF16),
            pltpu.VMEM((rank, rows), BF16),
            pltpu.VMEM((ff, rank), BF16),
            pltpu.VMEM((chunks, rank, CHUNK), F32),
            gcomm,
            gcomm, gcomm, gcomm, gcomm,
            comm, comm, comm, comm,
            dma((2, PIECES)), dma((2, PIECES)),
            dma((POWER + 1, 2, chunks)), dma((POWER + 1, 2, chunks)),
            dma((2, count // 2 - 1)), dma((2, count // 2 - 1)),
            dma,
        ],
        compiler_params=pltpu.CompilerParams(
            collective_id=0, has_side_effects=True, vmem_limit_bytes=VMEM_LIMIT),
        cost_estimate=pl.CostEstimate(
            flops=2 * rows * ff * rank * 6, bytes_accessed=rows * ff * 2, transcendentals=0),
        name="sketch_sums",
    )(deltas, weights)


def share_kernel(n, count, owner_ref, c_ref, yb_ref, c_out, y_out,
                 whole, piece, whole_send, whole_recv, piece_send, piece_recv, rows_z, y_send, y_recv,
                 wssem, wrsem, pssem, prsem, zssem, zrsem, bssem, brsem):
    me, own = lax.axis_index("fsdp"), lax.axis_index("ep")
    parity = lax.rem(own, 2)
    slots, rank, ff = c_out.shape
    half = ff // 2
    width = half // n
    bits = digits(count)
    stages = len(bits) - 1
    greet(me, n, own, bits)

    def slots_of(owner):
        seen, chosen, present = jnp.int32(0), [jnp.int32(0)] * slots, [jnp.int32(0)] * slots
        for expert in range(count):
            owned = (owner_ref[expert] == owner).astype(jnp.int32)
            for s in range(slots):
                hit = owned * (seen == s).astype(jnp.int32)
                chosen[s] = chosen[s] + hit * expert
                present[s] = present[s] + hit
            seen = seen + owned
        return chosen, present

    chosen, present = slots_of(own)
    other, _ = slots_of(flip(own, [0]))

    def beside(src, dst, index):
        return pltpu.make_async_remote_copy(
            src_ref=src, dst_ref=dst, send_sem=bssem.at[index], recv_sem=brsem.at[index],
            device_id={"ep": flip(own, [0])}, device_id_type=MESH)

    def for_partner(held, send):
        for s in range(slots):
            send[s] = held[lax.div(other[s], 2)]

    def mine(held, recv, s):
        return jnp.where(lax.rem(chosen[s], 2) == parity, held[lax.div(chosen[s], 2)], recv[s])

    whole[lax.div(own, 2)] = c_ref[:, :half]
    piece[lax.div(own, 2)] = c_ref[:, pl.ds(pl.multiple_of(half + me * width, width), width)]
    pieces = cubes(own, count, piece, pssem, prsem)
    wholes = cubes(own, count, whole, wssem, wrsem)
    for gather in pieces:
        gather.run(0)
    for gather in pieces:
        gather.run(1)
    for gather in wholes:
        gather.run(0)
    for_partner(yb_ref, y_send)
    y_copies = [beside(y_send.at[s], y_recv.at[s], 2 + s) for s in range(slots)]
    y_copies[0].start()
    for stage in range(2, stages + 1):
        for gather in pieces:
            gather.run(stage)
    for_partner(piece, piece_send)
    piece_copy = beside(piece_send, piece_recv, 1)
    piece_copy.start()
    for stage in range(1, stages):
        for gather in wholes:
            gather.run(stage)
    piece_copy.wait_recv()
    for s in range(slots):
        rows_z[me, s] = mine(piece, piece_recv, s)

    def right(block, hop):
        return pltpu.make_async_remote_copy(
            src_ref=rows_z.at[block], dst_ref=rows_z.at[block], send_sem=zssem.at[0, hop], recv_sem=zrsem.at[0, hop],
            device_id={"fsdp": jnp.minimum(me + 1, n - 1)}, device_id_type=MESH)

    def left(block, hop):
        return pltpu.make_async_remote_copy(
            src_ref=rows_z.at[block], dst_ref=rows_z.at[block], send_sem=zssem.at[1, hop], recv_sem=zrsem.at[1, hop],
            device_id={"fsdp": jnp.maximum(me - 1, 0)}, device_id_type=MESH)

    def send(hop, act):
        @pl.when((me - hop >= 0) & (me < n - 1))
        def _():
            act(right(me - hop, hop))

        @pl.when((me + hop <= n - 1) & (me > 0))
        def _():
            act(left(me + hop, hop))

    def receive(hop):
        @pl.when(me - 1 - hop >= 0)
        def _():
            right(me - 1 - hop, hop).wait_recv()

        @pl.when(me + 1 + hop <= n - 1)
        def _():
            left(me + 1 + hop, hop).wait_recv()

    send(0, lambda copy: copy.start())
    for copy in y_copies[1:]:
        copy.start()
    whole_copy = beside(whole_send, whole_recv, 0)
    for hop in range(n - 1):
        receive(hop)
        if hop < n - 2:
            send(hop + 1, lambda copy: copy.start())
        if hop == 0:
            for gather in wholes:
                gather.run(stages)
            for_partner(whole, whole_send)
            whole_copy.start()
    for s in range(slots):
        y_copies[s].wait_recv()
        y_out[s] = jnp.where(present[s] == 1, mine(yb_ref, y_recv, s), jnp.zeros_like(y_recv[s]))
    whole_copy.wait_recv()
    for s in range(slots):
        c_out[s, :, :half] = mine(whole, whole_recv, s)
        for z in range(n):
            c_out[s, :, half + z * width:half + (z + 1) * width] = rows_z[z, s]
    for gather in pieces + wholes:
        gather.finish()
    for copy in y_copies + [piece_copy, whole_copy]:
        copy.wait_send()
    for hop in range(n - 1):
        send(hop, lambda copy: copy.wait_send())


def share_call(n, count, slots, owner_of, coeffs, held):
    rank, ff = coeffs.shape
    rows = held.shape[1]
    half, width = ff // 2, ff // 2 // n
    vmem = pl.BlockSpec(memory_space=pltpu.VMEM)
    smem = pl.BlockSpec(memory_space=pltpu.SMEM)
    dma = pltpu.SemaphoreType.DMA
    return pl.pallas_call(
        functools.partial(share_kernel, n, count),
        out_shape=(
            jax.ShapeDtypeStruct((slots, rank, ff), BF16),
            jax.ShapeDtypeStruct((slots, rows, rank), BF16),
        ),
        in_specs=[smem, vmem, vmem],
        out_specs=(vmem, vmem),
        scratch_shapes=[
            pltpu.VMEM((count // 2, rank, half), BF16),
            pltpu.VMEM((count // 2, rank, width), BF16),
            pltpu.VMEM((slots, rank, half), BF16),
            pltpu.VMEM((slots, rank, half), BF16),
            pltpu.VMEM((slots, rank, width), BF16),
            pltpu.VMEM((slots, rank, width), BF16),
            pltpu.VMEM((n, slots, rank, width), BF16),
            pltpu.VMEM((slots, rows, rank), BF16),
            pltpu.VMEM((slots, rows, rank), BF16),
            dma((2, count // 2 - 1)), dma((2, count // 2 - 1)),
            dma((2, count // 2 - 1)), dma((2, count // 2 - 1)),
            dma((2, n - 1)), dma((2, n - 1)),
            dma((2 + slots,)), dma((2 + slots,)),
        ],
        compiler_params=pltpu.CompilerParams(
            collective_id=1, has_side_effects=True, vmem_limit_bytes=VMEM_LIMIT),
        name="share_chosen",
    )(owner_of, coeffs, held)


def mul(a, b):
    return jnp.dot(a, b, preferred_element_type=F32, precision=lax.Precision.HIGHEST)


def solve_kernel(gram_ref, cross_ref, out_ref, g_ref, x_ref):
    gram = gram_ref[...]
    rank = gram.shape[0]
    eye = lax.broadcasted_iota(jnp.int32, gram.shape, 0) == lax.broadcasted_iota(jnp.int32, gram.shape, 1)
    one = jnp.where(eye, F32(1), F32(0))
    diag = jnp.where(eye, gram, F32(0))
    down = lax.rsqrt(jnp.sum(diag, axis=1, keepdims=True))
    across = lax.rsqrt(jnp.sum(diag, axis=0, keepdims=True))
    g = gram * down * across
    g_ref[...] = g
    start = one / jnp.max(jnp.sum(jnp.abs(g), axis=1))
    x_ref[...] = start

    def rough(carry):
        count, _ = carry
        x = x_ref[...]
        low = x.astype(BF16)
        miss = one - jnp.dot(g_ref[...].astype(BF16), low, preferred_element_type=F32)
        x_ref[...] = x + jnp.dot(low, miss.astype(BF16), preferred_element_type=F32)
        return count + 1, jnp.sum(miss * miss)

    lax.while_loop(lambda c: (c[0] < 16) & (c[1] > 0.3), rough, (jnp.int32(0), F32(1e9)))
    miss = one - mul(g_ref[...], x_ref[...])
    sound = jnp.sum(miss * miss) < 0.9

    @pl.when(jnp.logical_not(sound))
    def _():
        x_ref[...] = start

    def newton(carry):
        count, _ = carry
        x = x_ref[...]
        miss = one - mul(g_ref[...], x)
        x_ref[...] = x + mul(x, miss)
        return count + 1, jnp.sum(miss * miss)

    lax.while_loop(lambda c: (c[0] < 64) & (c[1] > 1e-6), newton, (jnp.int32(0), F32(1e9)))
    out_ref[...] = (mul(x_ref[...], cross_ref[...] * down) * down).astype(BF16)


def solve_call(gram, cross):
    vmem = pl.BlockSpec(memory_space=pltpu.VMEM)
    return pl.pallas_call(
        solve_kernel,
        out_shape=jax.ShapeDtypeStruct(cross.shape, BF16),
        in_specs=[vmem, vmem],
        out_specs=vmem,
        scratch_shapes=[pltpu.VMEM(gram.shape, F32), pltpu.VMEM(gram.shape, F32)],
        compiler_params=pltpu.CompilerParams(vmem_limit_bytes=VMEM_LIMIT),
        cost_estimate=pl.CostEstimate(flops=10 * 10**9, bytes_accessed=10**6, transcendentals=0),
        name="solve",
    )(gram, cross)


def update_kernel(y_ref, c_ref, serving_ref, out_ref):
    tile, ff = y_ref.shape[1], c_ref.shape[2]
    for at in range(0, ff, 256):
        columns = slice(at, at + 256)
        for top in range(0, tile, tile // 2):
            rows = slice(top, top + tile // 2)
            update = jnp.dot(y_ref[0, rows, :], c_ref[0, :, columns], preferred_element_type=F32)
            out_ref[0, rows, columns] = (serving_ref[0, rows, columns].astype(F32) + update).astype(BF16)


def update_call(ys, coeffs, serving):
    slots, rows, ff = serving.shape
    rank = ys.shape[2]
    tile = rows // 2
    return pl.pallas_call(
        update_kernel,
        out_shape=jax.ShapeDtypeStruct(serving.shape, BF16),
        grid=(slots, rows // tile),
        in_specs=[
            pl.BlockSpec((1, tile, rank), lambda s, i: (s, i, 0)),
            pl.BlockSpec((1, rank, ff), lambda s, i: (s, 0, 0)),
            pl.BlockSpec((1, tile, ff), lambda s, i: (s, i, 0)),
        ],
        out_specs=pl.BlockSpec((1, tile, ff), lambda s, i: (s, i, 0)),
        compiler_params=pltpu.CompilerParams(vmem_limit_bytes=VMEM_LIMIT),
        cost_estimate=pl.CostEstimate(
            flops=2 * slots * rows * ff * rank, bytes_accessed=4 * slots * rows * ff, transcendentals=0),
        name="update",
    )(ys, coeffs, serving)


def local(n, count, deltas, sketch_matrix, owner_of, serving):
    gram, cross, held = sketch_call(n, count, deltas[0], sketch_matrix)
    coeffs, ys = share_call(n, count, serving.shape[0], owner_of, solve_call(gram, cross), held)
    return update_call(ys, coeffs, serving)


def solution(mesh):
    return jax.shard_map(
        functools.partial(local, mesh.shape["fsdp"], mesh.shape["ep"]),
        mesh=mesh,
        in_specs=(P("ep", "fsdp", None), P(), P(), P("ep", "fsdp", None)),
        out_specs=P("ep", "fsdp", None),
        check_vma=False,
    )
```
